512 devices in a mesh: head: 8 (over x, core), seq: 64 (over y, z).
Axes of the slice: x: 4, y: 4, z: 16, core: 2. Of those that a mesh axis runs over, the one named last changes fastest.
Arguments:
- queries: bfloat16 [64, 128, 2048], P('seq', 'head'), may hold values from -6 to 6
- key_inputs: bfloat16 [64, 128, 2048], P('seq', 'head'), may hold values from -6 to 6
- values: bfloat16 [64, 128, 2048], P('seq', 'head'), may hold values from -15 to 15
- beta_gates: float32 [16, 8192], P('head', 'seq'), may hold values from 0.0046875 to 0.98
- log_decay: float32 [16, 8192], P('head', 'seq'), as said below
- out_grad: bfloat16 [64, 128, 2048], P('seq', 'head'), may hold values from -6 to 6
Outputs:
- attended: bfloat16 [64, 128, 2048], P('seq', 'head')
- query_grad: float32 [64, 128, 2048], P('seq', 'head')
- key_grad: float32 [64, 128, 2048], P('seq', 'head')
- value_grad: float32 [64, 128, 2048], P('seq', 'head')
- beta_grad: float32 [16, 8192], P('head', 'seq')
- decay_grad: float32 [16, 8192], P('head', 'seq')
The draws below stay inside these ranges and needn't reach their ends.
Inputs may be any that keep to these rules, and one draw needn't show every extreme that they name: `log_decay`: every entry is negative.
All inputs are finite; a program needn't handle non-finite values.
Results may differ from the reference program's by a relative error of at most 0.0014.
Values may be sent and summed in bfloat16 or wider, within the bound.
A program may use at most 128 MiB of HBM per device.

```python
import jax
import jax.numpy as jnp
from jax import lax

HEADS = 16
KD = 128
VD = 128
BLOCK = 64
TOK_DEV = 128
TOKENS = 8192
N_SEQ = 64


def head_split(key, quick_share):
    return jax.random.randint(jax.random.fold_in(key, 5), (HEADS,), 0, 8) < quick_share


def draw_beta_gates(key, part):
    quick_share = 4
    quick = head_split(key, quick_share)
    key = jax.random.fold_in(key, 23)
    streams = jax.random.split(key, 2)
    lively = jnp.clip(jax.nn.sigmoid(1.5 * jax.random.normal(streams[0], (HEADS, TOKENS), jnp.float32)), 0.02, 0.98)
    gentle = jnp.exp(jax.random.uniform(streams[1], (HEADS, TOKENS), jnp.float32, jnp.log(0.3), jnp.log(1.0))) * KD / TOKENS
    return jnp.where(quick[:, None], lively, gentle).astype(jnp.float32)


def draw_log_decay(key, part):
    quick_share = 4
    spread = 2.0
    quick = head_split(key, quick_share)
    key = jax.random.fold_in(key, 11)
    streams = jax.random.split(key, 7)
    fast_rate = jnp.exp(jax.random.uniform(streams[1], (HEADS,), jnp.float32, jnp.log(1.0 / 50.0), jnp.log(1.0 / 20.0)))
    slow_rate = jnp.exp(jax.random.uniform(streams[2], (HEADS,), jnp.float32, jnp.log(0.05), jnp.log(0.2))) / TOKENS
    rates = jnp.where(quick, fast_rate, slow_rate)
    segment_factor = jnp.exp(jax.random.uniform(streams[3], (HEADS, TOKENS // TOK_DEV), jnp.float32, -jnp.log(spread), jnp.log(spread)))
    position_factor = jnp.exp(jax.random.uniform(streams[4], (HEADS, TOKENS), jnp.float32, -jnp.log(2.0), jnp.log(2.0)))
    damping_coefficient = -rates[:, None] * jnp.repeat(segment_factor, TOK_DEV, axis=1) * position_factor
    write_locations = jax.random.randint(streams[5], (HEADS, 2), 0, TOKENS)
    forget_logits = jnp.log(jax.random.uniform(streams[6], (HEADS, 2), jnp.float32, 0.5, 0.8))
    timestep_indices = jnp.arange(TOKENS, dtype=jnp.int32)
    write_strength_groups = jnp.sum(jnp.where(timestep_indices[None, :, None] == write_locations[:, None, :], forget_logits[:, None, :], 0.0), axis=2)
    return (damping_coefficient + write_strength_groups).astype(jnp.float32)


def levels(key, shape, pieces, low, top_value):
    def one(dim, parts):
        draws = jax.random.uniform(jax.random.fold_in(jax.random.fold_in(key, 6), dim), (parts,), jnp.float32, low / len(pieces), top_value / len(pieces))
        return jnp.repeat(jnp.exp(draws), shape[dim] // parts).reshape((-1,) + (1,) * (len(shape) - dim - 1))

    factor_of = one(*pieces[0])
    for cut in pieces[1:]:
        factor_of = factor_of * one(*cut)
    return factor_of


def scatter_about(stream_key, dims, deviation, reach, shards=(), held_as=jnp.bfloat16):
    level = levels(stream_key, dims, shards, -0.22, 0.18) if shards else 1.0
    values = jax.random.normal(stream_key, dims, jnp.float32) * deviation * level
    return jnp.minimum(jnp.maximum(values, -reach), reach).astype(held_as)


def setup_inputs(seed: int = 0) -> dict:
    seeds = jax.random.split(jax.random.key(seed), 7)
    queries = scatter_about(seeds[0], (N_SEQ, TOK_DEV, HEADS * KD), 1.0, 6.0, ((0, 64), (1, 8)))
    key_inputs = scatter_about(seeds[1], (N_SEQ, TOK_DEV, HEADS * KD), 1.0, 6.0, ((0, 64), (1, 8)))
    values = scatter_about(seeds[2], (N_SEQ, TOK_DEV, HEADS * VD), 2.5, 15.0, ((0, 64), (1, 8)))
    beta_gates = draw_beta_gates(jax.random.fold_in(seeds[6], 71), 0)
    log_decay = draw_log_decay(jax.random.fold_in(seeds[6], 71), 0)
    out_grad = scatter_about(seeds[5], (N_SEQ, TOK_DEV, HEADS * VD), 1.0, 6.0, ((0, 64), (1, 8)))
    return {"queries": queries, "key_inputs": key_inputs, "values": values, "beta_gates": beta_gates, "log_decay": log_decay, "out_grad": out_grad}


EPSILON = 1e-06
PRECISE = lax.Precision.HIGHEST

def product(left, right):
    return jnp.dot(left.astype(jnp.float32), right.astype(jnp.float32), precision=PRECISE, preferred_element_type=jnp.float32)

def unit_rows(matrix):
    return matrix / jnp.sqrt(lax.optimization_barrier(jnp.sum(matrix * matrix, axis=-1, keepdims=True)) + EPSILON)

def segment_split(key_rows, values, beta_rows, log_rows):
    block_len = key_rows.shape[0]
    row_ids = lax.broadcasted_iota(jnp.int32, (block_len, block_len), 0)
    col_ids = lax.broadcasted_iota(jnp.int32, (block_len, block_len), 1)
    lower_mask = (row_ids >= col_ids).astype(jnp.float32)
    strict = (row_ids > col_ids).astype(jnp.float32)
    cumulative = product(lower_mask, log_rows[:, None])[:, 0]
    decays = jnp.exp((cumulative[:, None] - cumulative[None, :]) * lower_mask) * lower_mask
    system = jnp.eye(block_len, dtype=jnp.float32) + strict * decays * beta_rows[:, None] * product(key_rows, key_rows.T)
    right_side = jnp.concatenate([beta_rows[:, None] * values, (beta_rows * jnp.exp(cumulative))[:, None] * key_rows], axis=1)
    solved = jax.scipy.linalg.solve_triangular(system, right_side, lower=True, unit_diagonal=True)
    value_width = values.shape[1]
    return (cumulative, decays, solved[:, :value_width], solved[:, value_width:])

def block_step(carried, sequence_pieces):
    queries, key_rows, values, beta_rows, log_rows = sequence_pieces
    cumulative, decays, fresh, weights = segment_split(key_rows, values, beta_rows, log_rows)
    corrected = fresh - product(weights, carried)
    scores = product(queries, key_rows.T) * decays
    outputs = jnp.exp(cumulative)[:, None] * product(queries, carried) + product(scores, corrected)
    last_log = cumulative[-1]
    tail_decay = jnp.exp(last_log - cumulative)
    carried = jnp.exp(last_log) * carried + product(key_rows.T, tail_decay[:, None] * corrected)
    return (carried, outputs)

def run_head(carried, queries, key_rows, values, beta_rows, log_rows):
    block_count = key_rows.shape[0] // BLOCK
    sequence_pieces = (queries.reshape(block_count, BLOCK, -1), key_rows.reshape(block_count, BLOCK, -1), values.reshape(block_count, BLOCK, -1), beta_rows.reshape(block_count, BLOCK), log_rows.reshape(block_count, BLOCK))
    carried, outputs = lax.scan(jax.checkpoint(block_step), carried, sequence_pieces)
    return (outputs.reshape(block_count * BLOCK, -1), carried)

def recurrent_kernel(queries, key_rows, values, beta_rows, log_rows):
    unit_q = unit_rows(queries)
    unit_k = unit_rows(key_rows)
    zero_states = jnp.zeros((HEADS, KD, VD), jnp.float32)
    outputs, _ = jax.vmap(run_head, in_axes=(0, 1, 1, 1, 0, 0), out_axes=(1, 0))(zero_states, unit_q, unit_k, values, beta_rows, log_rows)
    return outputs

def reference(queries, key_inputs, values, beta_gates, log_decay, out_grad):

    def as_heads(source, feature_width):
        return source.astype(jnp.float32).reshape(TOKENS, HEADS, feature_width)

    def to_blocks(source, feature_width):
        return source.reshape(N_SEQ, TOK_DEV, HEADS * feature_width)
    outputs, pullback = jax.vjp(recurrent_kernel, as_heads(queries, KD), as_heads(key_inputs, KD), as_heads(values, VD), beta_gates, log_decay)
    gradients = pullback(as_heads(out_grad, VD))
    return (to_blocks(outputs, VD).astype(jnp.bfloat16), to_blocks(gradients[0], KD), to_blocks(gradients[1], KD), to_blocks(gradients[2], VD), gradients[3], gradients[4])
```

```python
import functools

import jax
import jax.numpy as jnp
from jax import lax
from jax.experimental import pallas as pl
from jax.experimental.pallas import tpu as pltpu
from jax.sharding import PartitionSpec as P

D = 128
L = 128
EPSILON = 1e-06
F32, BF16 = jnp.float32, jnp.bfloat16
MESH = pl.DeviceIdType.MESH
NN = (((1,), (0,)), ((), ()))
NT = (((1,), (1,)), ((), ()))
TN = (((0,), (0,)), ((), ()))


def split(x):
    high = x.astype(BF16)
    return high, (x - high.astype(F32)).astype(BF16)


def dot(a, b, dims):
    return lax.dot_general(a, b, dims, preferred_element_type=F32)


def cat(parts, dim):
    return jnp.concatenate(parts, axis=dim)


def mm3(a, b, dims):
    ah, al = split(a)
    bh, bl = split(b)
    ca, cb = dims[0][0][0], dims[0][1][0]
    return dot(cat([ah, al, ah], ca), cat([bh, bh, bl], cb), dims)


def mm2l(a, b, dims):
    ah, al = split(a)
    ca, cb = dims[0][0][0], dims[0][1][0]
    return dot(cat([ah, al], ca), cat([b, b], cb), dims)


def mm2r(a, b, dims):
    bh, bl = split(b)
    ca, cb = dims[0][0][0], dims[0][1][0]
    return dot(cat([a, a], ca), cat([bh, bl], cb), dims)


def inverse_root(total):
    guess = lax.rsqrt(total)
    return guess * (1.5 - 0.5 * total * guess * guess)


def row_sum(x):
    return jnp.sum(x, axis=1, keepdims=True)


def column_sum(x):
    return jnp.sum(x, axis=0, keepdims=True)


def unit_lower_inverse(lower, rows, cols):
    def off_diagonal(size):
        place = (rows // (2 * size) == cols // (2 * size)) & (
            rows % (2 * size) >= size) & (cols % (2 * size) < size)
        return jnp.where(place, lower, 0.0)

    inverse = jnp.where(rows == cols, 1.0, 0.0) - off_diagonal(1)
    size = 2
    while size < L:
        inverse = inverse - mm3(mm3(inverse, off_diagonal(size), NN), inverse, NN)
        size *= 2
    return inverse


def block_front(q, k, v, g, beta_row, log_row, rows, cols):
    eye = rows == cols
    lower = rows >= cols

    def as_column(row):
        return row_sum(jnp.where(eye, row, 0.0))

    def as_row(column):
        return column_sum(jnp.where(eye, column, 0.0))

    beta = as_column(beta_row)
    total = row_sum(jnp.where(lower, log_row, 0.0))
    total_row = column_sum(jnp.where(rows <= cols, as_column(log_row), 0.0))
    decays = jnp.exp(jnp.where(lower, total - total_row, -1e30))
    last = total[L - 1:L, :]
    grown = jnp.exp(total)
    tail = jnp.exp(last - total)
    qf, kf = q.astype(F32), k.astype(F32)
    rq = inverse_root(row_sum(qf * qf) + EPSILON)
    rk = inverse_root(row_sum(kf * kf) + EPSILON)
    rk_row = as_row(rk)
    system = jnp.where(rows > cols, dot(k, k, NT) * (beta * rk) * (rk_row * decays), 0.0)
    scores = dot(q, k, NT) * rq * (rk_row * decays)
    inverse = unit_lower_inverse(system, rows, cols)
    fresh = mm2l(inverse * beta_row, v, NN)
    weights = mm2l(inverse * (beta_row * jnp.exp(total_row) * rk_row), k, NN)
    both = cat([weights, fresh], 1)
    seen = mm3(scores, both, NN)
    reach = qf * (rq * grown) - seen[:, :D]
    moved = mm2r(k, both * (tail * rk), TN)
    transition = jnp.where(eye, jnp.exp(last), 0.0) - moved[:, :D]
    injection = moved[:, D:]
    adjoint = mm2l(reach, g, TN)
    return dict(
        beta=beta, grown=grown, tail=tail, decays=decays, rq=rq, rk=rk, rk_row=rk_row,
        inverse=inverse, fresh=fresh, weights=weights, inner=seen[:, D:], reach=reach,
        back=mm2l(scores, g, TN), transition=transition, injection=injection, adjoint=adjoint)


def block_back(f, q, k, v, g, state, later, leaving, rows, cols):
    qf, kf, vf, gf = q.astype(F32), k.astype(F32), v.astype(F32), g.astype(F32)
    through = mm3(cat([f["weights"], f["reach"]], 0), state, NN)
    corrected = f["fresh"] - through[:L]
    outputs = through[L:] + f["inner"]
    rk, rq, beta, decays = f["rk"], f["rq"], f["beta"], f["decays"]
    d_corrected = f["back"] + (f["tail"] * rk) * mm2r(k, later, NN)
    d_right = mm3(f["inverse"], d_corrected, TN)
    d_value = beta * d_right
    d_beta = row_sum(d_right * corrected) / beta
    flow = row_sum(gf * outputs) - row_sum(d_value * vf)
    d_scores = mm2r(g, corrected, NT) * decays
    d_system = jnp.where(rows > cols, mm3(d_right, corrected, NT) * (beta * decays), 0.0)
    d_q = f["grown"] * mm2r(g, state, NT) + mm2l(d_scores * f["rk_row"], k, NN)
    d_k = (mm2l(d_scores * rq, q, TN) + f["tail"] * mm3(corrected, later, NT)
           - mm3(d_value * f["grown"], state, NT)
           - mm2l(d_system * f["rk_row"], k, NN) - mm2l(d_system * rk, k, TN))

    def norm_back(unit, scale, grad):
        return scale * (grad - unit * row_sum(unit * grad))

    d_beta_row = column_sum(jnp.where(rows == cols, d_beta, 0.0))
    d_log_row = column_sum(jnp.where(rows >= cols, flow, 0.0)) + leaving
    return (outputs, norm_back(qf * rq, rq, d_q), norm_back(kf * rk, rk, d_k), d_value,
            d_beta_row, d_log_row)


def layer_kernel(cfg, q_ref, k_ref, v_ref, g_ref, beta_ref, log_ref,
                 out16, out32, out_gates,
                 pack, landed, gate_pack, gate_landed, own, core_send, core_landed, core_state,
                 core_state_landed, prefix, row_parts, column_parts, running,
                 res16, res32, gate_res,
                 in_send, in_recv, gate_send, gate_recv, core_send_sem, core_recv_sem,
                 z_send, z_recv, y_send, y_recv, out_send, out_recv):
    X, Q, J, Y = cfg
    heads, lanes = X * Q, 2 * X
    rows_dev = L // lanes
    nb = Q // 2
    slots = nb * lanes
    hd, sq = lax.axis_index("head"), lax.axis_index("seq")
    x, c = hd // 2, hd % 2
    y, z = sq // (J * Q), sq % (J * Q)
    j, i = z // Q, z % Q
    base = y * (J * Q) + j * Q
    jj = jnp.where(c == 0, j, J - 1 - j)
    yy = jnp.where(c == 0, y, Y - 1 - y)
    at_home = i // nb == c

    def z_device(jj_other):
        place = jnp.where(c == 0, jj_other, J - 1 - jj_other)
        return (hd, y * (J * Q) + place * Q + i)

    def y_device(yy_other):
        place = jnp.where(c == 0, yy_other, Y - 1 - yy_other)
        return (hd, place * (J * Q) + z)

    partner = (x * 2 + 1 - c, sq)

    barrier = pltpu.get_barrier_semaphore()

    def greet_group(n, carry):
        there = (n // Q, base + n % Q)

        @pl.when((there[0] != hd) | (there[1] != sq))
        def _():
            pl.semaphore_signal(barrier, inc=1, device_id=there, device_id_type=MESH)
        return carry

    lax.fori_loop(0, lanes * Q, greet_group, 0)
    for step in range(1, J):
        pl.semaphore_signal(barrier, inc=1, device_id=z_device((jj + step) % J), device_id_type=MESH)
    for step in range(1, Y):
        pl.semaphore_signal(barrier, inc=1, device_id=y_device((yy + step) % Y), device_id_type=MESH)

    for h in range(heads):
        for n, ref in enumerate((q_ref, k_ref, v_ref, g_ref)):
            pack[h, n * rows_dev:(n + 1) * rows_dev, :] = ref[0, :, h * D:(h + 1) * D]
    for r in range(nb):
        gate_pack[r, 0:1, :] = beta_ref[r:r + 1, :]
        gate_pack[r, 1:2, :] = log_ref[r:r + 1, :]
    pl.semaphore_wait(barrier, lanes * Q - 1 + J - 1 + Y - 1)

    own_head = x * Q + i
    own_slot = (i % nb) * lanes + hd

    def send_head(n, carry):
        h = (own_head + 1 + n) % heads
        there = ((h // Q) * 2 + i // nb, base + h % Q)

        @pl.when((h != own_head) | jnp.logical_not(at_home))
        def _():
            pltpu.make_async_remote_copy(
                src_ref=pack.at[h], dst_ref=landed.at[own_slot], send_sem=in_send, recv_sem=in_recv,
                device_id=there, device_id_type=MESH).start()
        return carry

    lax.fori_loop(0, heads, send_head, 0)
    for r in range(nb):
        there = (x * 2 + i // nb, base + nb * c + r)
        here = at_home & (i % nb == r)

        @pl.when(jnp.logical_not(here))
        def _():
            pltpu.make_async_remote_copy(
                src_ref=gate_pack.at[r], dst_ref=gate_landed.at[i % nb], send_sem=gate_send,
                recv_sem=gate_recv, device_id=there, device_id_type=MESH).start()

        @pl.when(here)
        def _():
            gate_landed[i % nb] = gate_pack[r]

    @pl.when(at_home)
    def _():
        landed[own_slot] = pack[own_head]

    def settle(ref, count, sem):
        @pl.when(at_home)
        def _():
            part = ref.at[pl.ds(0, count - 1)]
            pltpu.make_async_copy(part, part, sem).wait()

        @pl.when(jnp.logical_not(at_home))
        def _():
            part = ref.at[pl.ds(0, count)]
            pltpu.make_async_copy(part, part, sem).wait()

    settle(landed, slots, in_recv)
    settle(gate_landed, nb, gate_recv)

    rows = lax.broadcasted_iota(jnp.int32, (L, L), 0)
    cols = lax.broadcasted_iota(jnp.int32, (L, L), 1)

    def operands(b):
        part = landed.at[b * lanes:(b + 1) * lanes]
        return [part[:, n * rows_dev:(n + 1) * rows_dev, :].reshape(L, D) for n in range(4)]

    fronts = []
    for b in range(nb):
        q, k, v, g = operands(b)
        fronts.append(block_front(q, k, v, g, gate_landed[b, 0:1, :], gate_landed[b, 1:2, :], rows, cols))

    first, second = fronts
    joined = mm3(second["transition"], cat([first["transition"], first["injection"]], 1), NN)
    transition = joined[:, :D]
    injection = joined[:, D:] + second["injection"]
    adjoint = mm3(first["transition"], second["adjoint"], TN) + first["adjoint"]

    up = c == 0
    flipped = transition.T
    own[0] = jnp.where(up, transition, flipped)
    own[1] = jnp.where(up, injection, adjoint)
    core_send[0] = jnp.where(up, flipped, transition)
    core_send[1] = jnp.where(up, adjoint, injection)
    core_copy = pltpu.make_async_remote_copy(
        src_ref=core_send, dst_ref=core_landed, send_sem=core_send_sem.at[0],
        recv_sem=core_recv_sem.at[0], device_id=partner, device_id_type=MESH)
    core_copy.start()
    core_copy.wait_recv()
    composed = mm3(core_landed[0], cat([own[0], own[1]], 1), NN)
    row_parts[jj, 0] = composed[:, :D]
    row_parts[jj, 1] = composed[:, D:] + core_landed[1]

    z_copies = []
    for step in range(1, J):
        copy = pltpu.make_async_remote_copy(
            src_ref=row_parts.at[jj], dst_ref=row_parts.at[jj], send_sem=z_send.at[step - 1],
            recv_sem=z_recv.at[step - 1], device_id=z_device((jj + step) % J), device_id_type=MESH)
        copy.start()
        z_copies.append(copy)
    for step in range(1, J):
        pltpu.make_async_copy(row_parts.at[0], row_parts.at[0], z_recv.at[step - 1]).wait()
    prefix[0, 0] = jnp.where(rows == cols, 1.0, 0.0)
    prefix[0, 1] = jnp.zeros((D, D), F32)
    a, b_ = row_parts[0, 0], row_parts[0, 1]
    for m in range(1, J):
        prefix[m, 0] = a
        prefix[m, 1] = b_
        joined = mm3(row_parts[m, 0], cat([a, b_], 1), NN)
        a, b_ = joined[:, :D], joined[:, D:] + row_parts[m, 1]

    column_parts[yy, 0] = a
    column_parts[yy, 1] = b_
    for step in range(1, Y):
        @pl.when(yy + step < Y)
        def _():
            pltpu.make_async_remote_copy(
                src_ref=column_parts.at[yy], dst_ref=column_parts.at[yy],
                send_sem=y_send.at[step - 1], recv_sem=y_recv.at[step - 1],
                device_id=y_device((yy + step) % Y), device_id_type=MESH).start()
    for step in range(1, Y):
        @pl.when(yy >= step)
        def _():
            pltpu.make_async_copy(column_parts.at[0], column_parts.at[0], y_recv.at[step - 1]).wait()
    running[...] = jnp.zeros((D, D), F32)
    for m in range(Y - 1):
        @pl.when(m < yy)
        def _():
            running[...] = mm3(column_parts[m, 0], running[...], NN) + column_parts[m, 1]
    entering = mm3(prefix[jj, 0], running[...], NN) + prefix[jj, 1]
    core_state[...] = mm3(own[0], entering, NN) + own[1]
    state_copy = pltpu.make_async_remote_copy(
        src_ref=core_state, dst_ref=core_state_landed, send_sem=core_send_sem.at[1],
        recv_sem=core_recv_sem.at[1], device_id=partner, device_id_type=MESH)
    state_copy.start()
    state_copy.wait_recv()
    other = core_state_landed[...]
    state = jnp.where(up, entering, other)
    later = jnp.where(up, other, entering)

    middle_state = mm3(first["transition"], state, NN) + first["injection"]
    middle_later = mm3(second["transition"], later, TN) + second["adjoint"]

    def inner(m, n):
        return column_sum(row_sum(m * n))

    leaving = (inner(middle_later, middle_state),
               inner(middle_later - second["adjoint"], middle_state) + inner(later, second["injection"]))
    for b, (f, s, n) in enumerate(((first, state, middle_later), (second, middle_state, later))):
        q, k, v, g = operands(b)
        outputs, d_q, d_k, d_v, d_beta, d_log = block_back(f, q, k, v, g, s, n, leaving[b], rows, cols)
        part16 = res16.at[b * lanes:(b + 1) * lanes]
        part32 = res32.at[b * lanes:(b + 1) * lanes]
        part16[...] = outputs.astype(BF16).reshape(lanes, rows_dev, D)
        for n_, grad in enumerate((d_q, d_k, d_v)):
            part32[:, n_ * rows_dev:(n_ + 1) * rows_dev, :] = grad.reshape(lanes, rows_dev, D)
        gate_res[b, 0:1, :] = d_beta
        gate_res[b, 1:2, :] = d_log

    def send_rows(n, carry):
        slot = (own_slot + 1 + n) % slots
        there = (slot % lanes, base + nb * c + slot // lanes)

        @pl.when((slot != own_slot) | jnp.logical_not(at_home))
        def _():
            pltpu.make_async_remote_copy(
                src_ref=res16.at[slot], dst_ref=out16.at[own_head], send_sem=out_send.at[0],
                recv_sem=out_recv.at[0], device_id=there, device_id_type=MESH).start()
            pltpu.make_async_remote_copy(
                src_ref=res32.at[slot], dst_ref=out32.at[own_head], send_sem=out_send.at[1],
                recv_sem=out_recv.at[1], device_id=there, device_id_type=MESH).start()
        return carry

    lax.fori_loop(0, slots, send_rows, 0)
    for m in range(nb):
        there = (x * 2 + i // nb, base + nb * c + m)
        here = at_home & (i % nb == m)

        @pl.when(jnp.logical_not(here))
        def _():
            pltpu.make_async_remote_copy(
                src_ref=gate_res.at[m], dst_ref=out_gates.at[i % nb], send_sem=out_send.at[2],
                recv_sem=out_recv.at[2], device_id=there, device_id_type=MESH).start()

        @pl.when(here)
        def _():
            out_gates[i % nb] = gate_res[m]

    @pl.when(at_home)
    def _():
        out16[own_head] = res16[own_slot]
        out32[own_head] = res32[own_slot]

    settle(out16, heads, out_recv.at[0])
    settle(out32, heads, out_recv.at[1])
    settle(out_gates, nb, out_recv.at[2])
    settle(pack, heads, in_send)
    settle(gate_pack, nb, gate_send)
    core_copy.wait_send()
    state_copy.wait_send()
    for copy in z_copies:
        copy.wait_send()
    for step in range(1, Y):
        @pl.when(yy + step < Y)
        def _():
            pltpu.make_async_copy(column_parts.at[0], column_parts.at[0], y_send.at[step - 1]).wait()
    settle(res16, slots, out_send.at[0])
    settle(res32, slots, out_send.at[1])
    settle(gate_res, nb, out_send.at[2])


def shards(cfg, queries, key_inputs, values, beta_gates, log_decay, out_grad):
    X, Q, J, Y = cfg
    heads, lanes = X * Q, 2 * X
    rows_dev = L // lanes
    nb = Q // 2
    slots = nb * lanes
    vmem = pl.BlockSpec(memory_space=pltpu.VMEM)
    dma = pltpu.SemaphoreType.DMA
    out16, out32, gates = pl.pallas_call(
        functools.partial(layer_kernel, cfg),
        out_shape=(
            jax.ShapeDtypeStruct((heads, rows_dev, D), BF16),
            jax.ShapeDtypeStruct((heads, 3 * rows_dev, D), F32),
            jax.ShapeDtypeStruct((nb, 8, L), F32),
        ),
        in_specs=[vmem] * 6,
        out_specs=(vmem, vmem, vmem),
        scratch_shapes=[
            pltpu.VMEM((heads, 4 * rows_dev, D), BF16),
            pltpu.VMEM((slots, 4 * rows_dev, D), BF16),
            pltpu.VMEM((nb, 8, L), F32),
            pltpu.VMEM((nb, 8, L), F32),
            pltpu.VMEM((2, D, D), F32),
            pltpu.VMEM((2, D, D), F32),
            pltpu.VMEM((2, D, D), F32),
            pltpu.VMEM((D, D), F32),
            pltpu.VMEM((D, D), F32),
            pltpu.VMEM((J, 2, D, D), F32),
            pltpu.VMEM((J, 2, D, D), F32),
            pltpu.VMEM((Y, 2, D, D), F32),
            pltpu.VMEM((D, D), F32),
            pltpu.VMEM((slots, rows_dev, D), BF16),
            pltpu.VMEM((slots, 3 * rows_dev, D), F32),
            pltpu.VMEM((nb, 8, L), F32),
            dma, dma, dma, dma, dma((2,)), dma((2,)),
            dma((J - 1,)), dma((J - 1,)), dma((Y - 1,)), dma((Y - 1,)), dma((3,)), dma((3,)),
        ],
        compiler_params=pltpu.CompilerParams(
            collective_id=0, has_side_effects=True, vmem_limit_bytes=40 * 1024 * 1024),
        name="delta_rule",
    )(queries, key_inputs, values, out_grad, beta_gates, log_decay)

    def as_rows(landed):
        return jnp.transpose(landed, (1, 0, 2)).reshape(1, rows_dev, heads * D)

    grads = [as_rows(out32[:, n * rows_dev:(n + 1) * rows_dev]) for n in range(3)]
    return (as_rows(out16), *grads, gates[:, 0], gates[:, 1])


def build(mesh, y_chips):
    X = mesh.shape["head"] // 2
    heads = 16 if y_chips == 4 else 4 * X
    Q = heads // X
    J = mesh.shape["seq"] // (y_chips * Q)
    rows = P("seq", "head", None)
    gates = P("head", "seq")
    return jax.shard_map(
        functools.partial(shards, (X, Q, J, y_chips)), mesh=mesh,
        in_specs=(rows, rows, rows, gates, gates, rows),
        out_specs=(rows, rows, rows, rows, gates, gates), check_vma=False)


def solution(mesh):
    return build(mesh, 4)
```

```python
import functools

import jax
import jax.numpy as jnp
from jax import lax
from jax.experimental import pallas as pl
from jax.experimental.pallas import tpu as pltpu
from jax.sharding import PartitionSpec as P

D = 128
L = 128
EPSILON = 1e-06
F32, BF16 = jnp.float32, jnp.bfloat16
MESH = pl.DeviceIdType.MESH
NN = (((1,), (0,)), ((), ()))
NT = (((1,), (1,)), ((), ()))
TN = (((0,), (0,)), ((), ()))


def split(x):
    high = x.astype(BF16)
    return high, (x - high.astype(F32)).astype(BF16)


def dot(a, b, dims):
    return lax.dot_general(a, b, dims, preferred_element_type=F32)


def cat(parts, dim):
    return jnp.concatenate(parts, axis=dim)


def mm3(a, b, dims):
    ah, al = split(a)
    bh, bl = split(b)
    ca, cb = dims[0][0][0], dims[0][1][0]
    return dot(cat([ah, al, ah], ca), cat([bh, bh, bl], cb), dims)


def mm2l(a, b, dims):
    ah, al = split(a)
    ca, cb = dims[0][0][0], dims[0][1][0]
    return dot(cat([ah, al], ca), cat([b, b], cb), dims)


def mm2r(a, b, dims):
    bh, bl = split(b)
    ca, cb = dims[0][0][0], dims[0][1][0]
    return dot(cat([a, a], ca), cat([bh, bl], cb), dims)


def inverse_root(total):
    guess = lax.rsqrt(total)
    return guess * (1.5 - 0.5 * total * guess * guess)


def row_sum(x):
    return jnp.sum(x, axis=1, keepdims=True)


def column_sum(x):
    return jnp.sum(x, axis=0, keepdims=True)


def unit_lower_inverse(lower, rows, cols):
    def off_diagonal(size):
        place = (rows // (2 * size) == cols // (2 * size)) & (
            rows % (2 * size) >= size) & (cols % (2 * size) < size)
        return jnp.where(place, lower, 0.0)

    inverse = jnp.where(rows == cols, 1.0, 0.0) - off_diagonal(1)
    size = 2
    while size < L:
        inverse = inverse - mm3(mm3(inverse, off_diagonal(size), NN), inverse, NN)
        size *= 2
    return inverse


def block_front(k, v, beta_row, log_row, rows, cols):
    eye = rows == cols
    lower = rows >= cols

    def as_column(row):
        return row_sum(jnp.where(eye, row, 0.0))

    def as_row(column):
        return column_sum(jnp.where(eye, column, 0.0))

    beta = as_column(beta_row)
    total = row_sum(jnp.where(lower, log_row, 0.0))
    total_row = column_sum(jnp.where(rows <= cols, as_column(log_row), 0.0))
    decays = jnp.exp(jnp.where(lower, total - total_row, -1e30))
    last = total[L - 1:L, :]
    grown = jnp.exp(total)
    tail = jnp.exp(last - total)
    kf = k.astype(F32)
    rk = inverse_root(row_sum(kf * kf) + EPSILON)
    rk_row = as_row(rk)
    system = jnp.where(rows > cols, dot(k, k, NT) * (beta * rk) * (rk_row * decays), 0.0)
    inverse = unit_lower_inverse(system, rows, cols)
    fresh = mm2l(inverse * beta_row, v, NN)
    weights = mm2l(inverse * (beta_row * jnp.exp(total_row) * rk_row), k, NN)
    both = cat([weights, fresh], 1)
    moved = mm2l(both * (tail * rk), k, TN)
    transition = jnp.where(eye, jnp.exp(last), 0.0) - moved[:D]
    return dict(
        beta=beta, grown=grown, tail=tail, decays=decays, rk=rk, rk_row=rk_row, inverse=inverse,
        fresh=fresh, weights=weights, both=both, transition=transition, injection=moved[D:])


def block_reach(f, q, k, g):
    qf = q.astype(F32)
    rq = inverse_root(row_sum(qf * qf) + EPSILON)
    scores = dot(q, k, NT) * rq * (f["rk_row"] * f["decays"])
    seen = mm3(scores, f["both"], NN)
    reach = qf * (rq * f["grown"]) - seen[:, :D]
    return dict(
        rq=rq, inner=seen[:, D:], reach=reach, back=mm2l(scores, g, TN), adjoint=mm2r(g, reach, TN))


def block_back(f, q, k, v, g, state, later, leaving, rows, cols):
    qf, kf, vf, gf = q.astype(F32), k.astype(F32), v.astype(F32), g.astype(F32)
    through = mm3(cat([f["weights"], f["reach"]], 0), state, NT)
    corrected = f["fresh"] - through[:L]
    outputs = through[L:] + f["inner"]
    rk, rq, beta, decays = f["rk"], f["rq"], f["beta"], f["decays"]
    d_corrected = f["back"] + (f["tail"] * rk) * mm2r(k, later, NT)
    d_right = mm3(f["inverse"], d_corrected, TN)
    d_value = beta * d_right
    d_beta = row_sum(d_right * corrected) / beta
    flow = row_sum(gf * outputs) - row_sum(d_value * vf)
    d_scores = mm2r(g, corrected, NT) * decays
    d_system = jnp.where(rows > cols, mm3(d_right, corrected, NT) * (beta * decays), 0.0)
    d_q = f["grown"] * mm2r(g, state, NN) + mm2l(d_scores * f["rk_row"], k, NN)
    d_k = (mm2l(d_scores * rq, q, TN) + f["tail"] * mm3(corrected, later, NN)
           - mm3(d_value * f["grown"], state, NN)
           - mm2l(d_system * f["rk_row"], k, NN) - mm2l(d_system * rk, k, TN))

    def norm_back(unit, scale, grad):
        return scale * (grad - unit * row_sum(unit * grad))

    d_beta_row = column_sum(jnp.where(rows == cols, d_beta, 0.0))
    d_log_row = column_sum(jnp.where(rows >= cols, flow, 0.0)) + leaving
    return (outputs, norm_back(qf * rq, rq, d_q), norm_back(kf * rk, rk, d_k), d_value,
            d_beta_row, d_log_row)


def layer_kernel(cfg, q_hbm, k_hbm, v_hbm, g_hbm, beta_hbm, log_hbm,
                 out16, out32, out_gates,
                 q_ref, k_ref, v_ref, g_ref, beta_ref, log_ref, pack_kv, pack_qg, landed_kv, landed_qg,
                 gate_pack, gate_landed, own, other, z_steps, i_parts, j_parts, z_i, z_j,
                 y_up, y_down, from_lower, from_upper, forward, backward, ret, ret_landed,
                 hand, held, res16, res32, gate_res,
                 load_sem, in_send, in_recv, core_send, core_recv,
                 z_send, z_recv, y_send, y_recv, ret_send, ret_recv, out_send, out_recv):
    X, Q, J, Y = cfg
    heads, lanes = X * Q, 2 * X
    rows_dev = L // lanes
    nb = Q // 2
    slots = nb * lanes
    part = D // J
    hd, sq = lax.axis_index("head"), lax.axis_index("seq")
    x, c = hd // 2, hd % 2
    y, z = sq // (J * Q), sq % (J * Q)
    j, i = z // Q, z % Q
    base = y * (J * Q) + j * Q
    at_home = i // nb == c
    scans = c == 0
    helps = c == 1
    partner = (x * 2 + 1 - c, sq)

    def remote(src, dst, send, recv, there):
        return pltpu.make_async_remote_copy(
            src_ref=src, dst_ref=dst, send_sem=send, recv_sem=recv, device_id=there, device_id_type=MESH)

    def await_bytes(ref, sem):
        pltpu.make_async_copy(ref, ref, sem).wait()

    def z_device(place):
        return (hd, y * (J * Q) + place * Q + i)

    def y_device(place):
        return (hd, place * (J * Q) + z)

    loads = [pltpu.make_async_copy(src, dst, load_sem.at[n]) for n, (src, dst) in enumerate((
        (k_hbm, k_ref), (v_hbm, v_ref), (beta_hbm, beta_ref), (log_hbm, log_ref),
        (q_hbm, q_ref), (g_hbm, g_ref)))]
    for load in loads:
        load.start()

    barrier = pltpu.get_barrier_semaphore()

    def greet_group(n, carry):
        there = (n // Q, base + n % Q)

        @pl.when((there[0] != hd) | (there[1] != sq))
        def _():
            pl.semaphore_signal(barrier, inc=1, device_id=there, device_id_type=MESH)
        return carry

    lax.fori_loop(0, lanes * Q, greet_group, 0)

    @pl.when(scans)
    def _():
        for step in range(1, J):
            pl.semaphore_signal(
                barrier, inc=1, device_id=z_device((j + step) % J), device_id_type=MESH)
        for step in range(1, Y):
            pl.semaphore_signal(
                barrier, inc=1, device_id=y_device((y + step) % Y), device_id_type=MESH)

    for load in loads:
        load.wait()
    for h in range(heads):
        for pack, refs in ((pack_kv, (k_ref, v_ref)), (pack_qg, (q_ref, g_ref))):
            for n, ref in enumerate(refs):
                pack[h, n * rows_dev:(n + 1) * rows_dev, :] = ref[0, :, h * D:(h + 1) * D]
    for r in range(nb):
        gate_pack[r, 0:1, :] = beta_ref[r:r + 1, :]
        gate_pack[r, 1:2, :] = log_ref[r:r + 1, :]

    @pl.when(scans)
    def _():
        pl.semaphore_wait(barrier, lanes * Q - 1 + J - 1 + Y - 1)

    @pl.when(helps)
    def _():
        pl.semaphore_wait(barrier, lanes * Q - 1)

    own_head = x * Q + i
    own_slot = (i % nb) * lanes + hd

    def send_rows_in(pack, landed, n):
        def send(m, carry):
            there_x, there_i = x ^ (X - 1 - m % X), i ^ (Q - 1 - m // X)

            @pl.when((m != heads - 1) | jnp.logical_not(at_home))
            def _():
                remote(pack.at[there_x * Q + there_i], landed.at[own_slot], in_send.at[n],
                       in_recv.at[n], (there_x * 2 + i // nb, base + there_i)).start()
            return carry

        lax.fori_loop(0, heads, send, 0)

        @pl.when(at_home)
        def _():
            landed[own_slot] = pack[own_head]

    for r in range(nb):
        there = (x * 2 + i // nb, base + nb * c + r)
        here = at_home & (i % nb == r)

        @pl.when(jnp.logical_not(here))
        def _():
            remote(gate_pack.at[r], gate_landed.at[i % nb], in_send.at[2], in_recv.at[2], there).start()

        @pl.when(here)
        def _():
            gate_landed[i % nb] = gate_pack[r]

    send_rows_in(pack_kv, landed_kv, 0)
    send_rows_in(pack_qg, landed_qg, 1)

    def settle(ref, count, sem):
        @pl.when(at_home)
        def _():
            await_bytes(ref.at[pl.ds(0, count - 1)], sem)

        @pl.when(jnp.logical_not(at_home))
        def _():
            await_bytes(ref.at[pl.ds(0, count)], sem)

    rows = lax.broadcasted_iota(jnp.int32, (L, L), 0)
    cols = lax.broadcasted_iota(jnp.int32, (L, L), 1)

    def operands(b, landed):
        part_ = landed.at[b * lanes:(b + 1) * lanes]
        return [part_[:, n * rows_dev:(n + 1) * rows_dev, :].reshape(L, D) for n in range(2)]

    settle(gate_landed, nb, in_recv.at[2])
    settle(landed_kv, slots, in_recv.at[0])
    blocks = []
    for b in range(nb):
        k, v = operands(b, landed_kv)
        blocks.append(block_front(k, v, gate_landed[b, 0:1, :], gate_landed[b, 1:2, :], rows, cols))
    first, second = blocks
    joined = mm3(cat([first["transition"], first["injection"]], 0), second["transition"], NN)
    own[0] = joined[:D]
    own[1] = joined[D:] + second["injection"]

    @pl.when(helps)
    def _():
        remote(own.at[pl.ds(0, 2)], other.at[pl.ds(0, 2)], core_send.at[0], core_recv.at[0], partner).start()

    settle(landed_qg, slots, in_recv.at[1])

    def reach(b):
        q, g = operands(b, landed_qg)
        blocks[b].update(block_reach(blocks[b], q, operands(b, landed_kv)[0], g))

    reach(0)

    @pl.when(scans)
    def _():
        await_bytes(other.at[pl.ds(0, 2)], core_recv.at[0])
        chip = mm3(cat([own[0], own[1]], 0), other[0], NN)
        z_steps[j] = chip[:D]
        for step in range(1, J):
            remote(z_steps.at[j], z_steps.at[j], z_send.at[0, step - 1], z_recv.at[0, step - 1],
                   z_device((j + step) % J)).start()
        i_parts[...] = (chip[D:] + other[1]).reshape(J, part, D)
        for step in range(1, J):
            remote(i_parts.at[(j + step) % J], z_i.at[j], z_send.at[1, step - 1],
                   z_recv.at[1, step - 1], z_device((j + step) % J)).start()
        z_i[j] = i_parts[j]

    reach(1)
    own[2] = mm3(second["adjoint"], first["transition"], NT) + first["adjoint"]

    @pl.when(helps)
    def _():
        remote(own.at[2], other.at[2], core_send.at[1], core_recv.at[1], partner).start()

    @pl.when(scans)
    def _():
        await_bytes(other.at[2], core_recv.at[1])
        j_parts[...] = (mm3(other[2], own[0], NT) + own[2]).reshape(J, part, D)
        for step in range(1, J):
            remote(j_parts.at[(j + step) % J], z_j.at[j], z_send.at[2, step - 1],
                   z_recv.at[2, step - 1], z_device((j + step) % J)).start()
        z_j[j] = j_parts[j]
        for step in range(1, J):
            await_bytes(z_steps.at[0], z_recv.at[0, step - 1])
            await_bytes(z_i.at[0], z_recv.at[1, step - 1])
        run = cat([z_steps[0], z_i[0]], 0)
        for m in range(1, J):
            run = mm3(run, z_steps[m], NN)
            run = cat([run[:D], run[D:] + z_i[m]], 0)
        y_up[...] = run
        y_down[0:D, :] = run[:D]
        for step in range(1, J):
            await_bytes(z_j.at[0], z_recv.at[2, step - 1])
        run = z_j[J - 1]
        for m in range(J - 2, -1, -1):
            run = mm3(run, z_steps[m], NT) + z_j[m]
        y_down[D:, :] = run

        for step in range(1, Y):
            place = (y + step) % Y

            @pl.when(place > y)
            def _():
                remote(y_up, from_lower.at[y], y_send.at[step - 1], y_recv.at[step - 1],
                       y_device(place)).start()

            @pl.when(place < y)
            def _():
                remote(y_down, from_upper.at[y], y_send.at[step - 1], y_recv.at[step - 1],
                       y_device(place)).start()
        for step in range(1, Y):
            await_bytes(from_lower.at[0], y_recv.at[step - 1])
        forward[...] = jnp.zeros((part, D), F32)
        backward[...] = jnp.zeros((part, D), F32)
        for m in range(Y - 1):
            @pl.when(m < y)
            def _():
                forward[...] = mm3(forward[...], from_lower[m, 0:D, :], NN) + from_lower[m, D:, :]

            @pl.when(Y - 1 - m > y)
            def _():
                backward[...] = (mm3(backward[...], from_upper[Y - 1 - m, 0:D, :], NT)
                                 + from_upper[Y - 1 - m, D:, :])

        up, down = forward[...], backward[...]
        for m in range(J):
            ret[m, 0] = up
            ret[J - 1 - m, 1] = down
            if m < J - 1:
                up = mm3(up, z_steps[m], NN) + z_i[m]
                down = mm3(down, z_steps[J - 1 - m], NT) + z_j[J - 1 - m]
        for step in range(1, J):
            place = (j + step) % J
            remote(ret.at[place], ret_landed.at[j], ret_send.at[step - 1], ret_recv.at[step - 1],
                   z_device(place)).start()
        ret_landed[j] = ret[j]
        for step in range(1, J):
            await_bytes(ret_landed.at[0], ret_recv.at[step - 1])
        hand[0] = ret_landed[:, 1].reshape(D, D)
        remote(hand.at[0], held.at[0], core_send.at[0], core_recv.at[0], partner).start()
        held[1] = ret_landed[:, 0].reshape(D, D)
        hand[1] = mm3(held[1], own[0], NN) + own[1]
        remote(hand.at[1], held.at[1], core_send.at[1], core_recv.at[1], partner).start()
        held[0] = mm3(hand[0], other[0], NT) + other[2]

    @pl.when(helps)
    def _():
        await_bytes(held.at[0], core_recv.at[0])
        await_bytes(held.at[1], core_recv.at[1])

    later, state = held[0], held[1]

    middle_state = mm3(state, first["transition"], NN) + first["injection"]
    middle_later = mm3(later, second["transition"], NT) + second["adjoint"]

    def inner(m, n):
        return column_sum(row_sum(m * n))

    leaving = (inner(middle_later, middle_state),
               inner(middle_later - second["adjoint"], middle_state) + inner(later, second["injection"]))
    for b, (f, s, n) in enumerate(((first, state, middle_later), (second, middle_state, later))):
        k, v = operands(b, landed_kv)
        q, g = operands(b, landed_qg)
        outputs, d_q, d_k, d_v, d_beta, d_log = block_back(f, q, k, v, g, s, n, leaving[b], rows, cols)
        res16[b * lanes:(b + 1) * lanes] = outputs.astype(BF16).reshape(lanes, rows_dev, D)
        for n_, grad in enumerate((d_q, d_k, d_v)):
            res32[b * lanes:(b + 1) * lanes, n_ * rows_dev:(n_ + 1) * rows_dev, :] = grad.reshape(
                lanes, rows_dev, D)
        gate_res[b, 0:1, :] = d_beta
        gate_res[b, 1:2, :] = d_log

    def send_rows_back(m, carry):
        slot = own_slot ^ (slots - 1 - m)
        there = (slot % lanes, base + nb * c + slot // lanes)

        @pl.when((m != slots - 1) | jnp.logical_not(at_home))
        def _():
            remote(res32.at[slot], out32.at[own_head], out_send.at[1], out_recv.at[1], there).start()
            remote(res16.at[slot], out16.at[own_head], out_send.at[0], out_recv.at[0], there).start()
        return carry

    lax.fori_loop(0, slots, send_rows_back, 0)
    for m in range(nb):
        there = (x * 2 + i // nb, base + nb * c + m)
        here = at_home & (i % nb == m)

        @pl.when(jnp.logical_not(here))
        def _():
            remote(gate_res.at[m], out_gates.at[i % nb], out_send.at[2], out_recv.at[2], there).start()

        @pl.when(here)
        def _():
            out_gates[i % nb] = gate_res[m]

    @pl.when(at_home)
    def _():
        out16[own_head] = res16[own_slot]
        out32[own_head] = res32[own_slot]

    settle(pack_kv, heads, in_send.at[0])
    settle(pack_qg, heads, in_send.at[1])
    settle(gate_pack, nb, in_send.at[2])

    @pl.when(helps)
    def _():
        await_bytes(own.at[pl.ds(0, 2)], core_send.at[0])
        await_bytes(own.at[2], core_send.at[1])

    @pl.when(scans)
    def _():
        await_bytes(hand.at[0], core_send.at[0])
        await_bytes(hand.at[1], core_send.at[1])
        for step in range(1, J):
            await_bytes(z_steps.at[0], z_send.at[0, step - 1])
            await_bytes(i_parts.at[0], z_send.at[1, step - 1])
            await_bytes(j_parts.at[0], z_send.at[2, step - 1])
            await_bytes(ret.at[0], ret_send.at[step - 1])
        for step in range(1, Y):
            await_bytes(y_up, y_send.at[step - 1])

    settle(out_gates, nb, out_recv.at[2])
    settle(out16, heads, out_recv.at[0])
    settle(out32, heads, out_recv.at[1])
    settle(res16, slots, out_send.at[0])
    settle(res32, slots, out_send.at[1])
    settle(gate_res, nb, out_send.at[2])


def unpack_kernel(in16, in32, in_gates, att, d_q, d_k, d_v, d_beta, d_log, wide16, wide32, gates, sems):
    heads, rows_dev, _ = in16.shape
    copies = []
    for n, out in enumerate((d_q, d_k, d_v)):
        for h in range(heads):
            wide32[n, :, h * D:(h + 1) * D] = in32[h, n * rows_dev:(n + 1) * rows_dev, :]
        copies.append(pltpu.make_async_copy(wide32.at[n], out.at[0], sems.at[n]))
        copies[-1].start()
    for h in range(heads):
        wide16[:, h * D:(h + 1) * D] = in16[h]
    copies.append(pltpu.make_async_copy(wide16, att.at[0], sems.at[3]))
    copies[-1].start()
    for n, out in enumerate((d_beta, d_log)):
        for r in range(in_gates.shape[0]):
            gates[n, r:r + 1, :] = in_gates[r, n:n + 1, :]
        copies.append(pltpu.make_async_copy(gates.at[n], out, sems.at[4 + n]))
        copies[-1].start()
    for copy in copies:
        copy.wait()


def shards(cfg, queries, key_inputs, values, beta_gates, log_decay, out_grad):
    X, Q, J, Y = cfg
    heads, lanes = X * Q, 2 * X
    rows_dev = L // lanes
    nb = Q // 2
    slots = nb * lanes
    part = D // J
    vmem = pl.BlockSpec(memory_space=pltpu.VMEM)
    hbm = pl.BlockSpec(memory_space=pl.ANY)
    dma = pltpu.SemaphoreType.DMA

    def wide(shape, kind=F32):
        return pltpu.VMEM(shape, kind)

    landed = pl.pallas_call(
        functools.partial(layer_kernel, cfg),
        out_shape=(
            jax.ShapeDtypeStruct((heads, rows_dev, D), BF16),
            jax.ShapeDtypeStruct((heads, 3 * rows_dev, D), F32),
            jax.ShapeDtypeStruct((nb, 8, L), F32),
        ),
        in_specs=[hbm] * 6,
        out_specs=(vmem, vmem, vmem),
        scratch_shapes=[
            *[wide((1, rows_dev, heads * D), BF16)] * 4, wide((nb, L)), wide((nb, L)),
            *[wide((heads, 2 * rows_dev, D), BF16)] * 2, *[wide((slots, 2 * rows_dev, D), BF16)] * 2,
            wide((nb, 8, L)), wide((nb, 8, L)), wide((3, D, D)), wide((3, D, D)),
            wide((J, D, D)), *[wide((J, part, D))] * 4,
            *[wide((D + part, D))] * 2, *[wide((Y, D + part, D))] * 2, *[wide((part, D))] * 2,
            *[wide((J, 2, part, D))] * 2, wide((2, D, D)), wide((2, D, D)),
            wide((slots, rows_dev, D), BF16), wide((slots, 3 * rows_dev, D)), wide((nb, 8, L)),
            dma((6,)), dma((3,)), dma((3,)), dma((2,)), dma((2,)),
            dma((3, J - 1)), dma((3, J - 1)), dma((Y - 1,)), dma((Y - 1,)),
            dma((J - 1,)), dma((J - 1,)), dma((3,)), dma((3,)),
        ],
        compiler_params=pltpu.CompilerParams(
            collective_id=0, has_side_effects=True, vmem_limit_bytes=48 * 1024 * 1024),
        name="delta_rule",
    )(queries, key_inputs, values, out_grad, beta_gates, log_decay)
    rows = jax.ShapeDtypeStruct((1, rows_dev, heads * D), F32)
    gates = jax.ShapeDtypeStruct((nb, L), F32)
    return pl.pallas_call(
        unpack_kernel,
        out_shape=(jax.ShapeDtypeStruct(rows.shape, BF16), rows, rows, rows, gates, gates),
        in_specs=[vmem] * 3,
        out_specs=(hbm,) * 6,
        scratch_shapes=[
            wide((rows_dev, heads * D), BF16), wide((3, rows_dev, heads * D)), wide((2, nb, L)), dma((6,))],
        name="unpack",
    )(*landed)


def build(mesh, y_chips):
    X = mesh.shape["head"] // 2
    heads = 16 if y_chips == 4 else 4 * X
    Q = heads // X
    J = mesh.shape["seq"] // (y_chips * Q)
    rows = P("seq", "head", None)
    gates = P("head", "seq")
    return jax.shard_map(
        functools.partial(shards, (X, Q, J, y_chips)), mesh=mesh,
        in_specs=(rows, rows, rows, gates, gates, rows),
        out_specs=(rows, rows, rows, rows, gates, gates), check_vma=False)


def solution(mesh):
    return build(mesh, 4)
```

```python
import functools
import math

import jax
import jax.numpy as jnp
from jax import lax
from jax.experimental import pallas as pl
from jax.experimental.pallas import tpu as pltpu
from jax.sharding import PartitionSpec as P

D = 128
L = 128
EPSILON = 1e-06
SPAN = 240.0
F32, BF16 = jnp.float32, jnp.bfloat16
MESH = pl.DeviceIdType.MESH
NN = (((1,), (0,)), ((), ()))
NT = (((1,), (1,)), ((), ()))
TN = (((0,), (0,)), ((), ()))


def split(x):
    high = x.astype(BF16)
    return high, (x - high.astype(F32)).astype(BF16)


def dot(a, b, dims):
    return lax.dot_general(a, b, dims, preferred_element_type=F32)


def cat(parts, dim):
    return jnp.concatenate(parts, axis=dim)


def mm3(a, b, dims):
    ah, al = split(a)
    bh, bl = split(b)
    ca, cb = dims[0][0][0], dims[0][1][0]
    return dot(cat([ah, al, ah], ca), cat([bh, bh, bl], cb), dims)


def mm2l(a, b, dims):
    ah, al = split(a)
    ca, cb = dims[0][0][0], dims[0][1][0]
    return dot(cat([ah, al], ca), cat([b, b], cb), dims)


def mm2r(a, b, dims):
    bh, bl = split(b)
    ca, cb = dims[0][0][0], dims[0][1][0]
    return dot(cat([a, a], ca), cat([bh, bl], cb), dims)


def inverse_root(total):
    guess = lax.rsqrt(total)
    return guess * (1.5 - 0.5 * total * guess * guess)


def row_sum(x):
    return jnp.sum(x, axis=1, keepdims=True)


def column_sum(x):
    return jnp.sum(x, axis=0, keepdims=True)


def encode(values, dim=0):
    scale = (jnp.maximum(jnp.max(jnp.abs(values), axis=dim, keepdims=True), 1e-30) * 1.01).astype(BF16)
    scale = scale.astype(F32)
    code = jnp.exp2(jnp.abs(values) * (SPAN / scale) - SPAN / 2)
    return jnp.where(values < 0, -code, code).astype(BF16), scale


def decode(code, scale):
    code = code.astype(F32)
    size = (jnp.log(jnp.abs(code)) * (1 / math.log(2)) + SPAN / 2) * (scale / SPAN)
    return jnp.where(code < 0, -size, size)


def scale_rows(scales):
    shape = scales[0].shape[:-2] + (16, D)
    row = lax.broadcasted_iota(jnp.int32, shape, len(shape) - 2)
    tile = jnp.zeros(shape, F32)
    for n, scale in enumerate(scales):
        tile = jnp.where(row == n, scale, tile)
    return tile.astype(BF16)


def encode_transition(transition, eye):
    diagonal = column_sum(row_sum(jnp.where(eye, transition, 0.0))) / D
    diagonal = diagonal.astype(BF16).astype(F32)
    code, scale = encode(transition - jnp.where(eye, diagonal, 0.0))
    return code, scale, diagonal


def put_step(ref, coded_transition, shift):
    code, scale, diagonal = coded_transition
    ref[0:D, :] = code
    code, shift_scale = encode(shift)
    ref[D:2 * D, :] = code
    ref[2 * D:2 * D + 16, :] = scale_rows([scale, shift_scale, diagonal])


def decode_step(ref, eye):
    tile = ref[2 * D:2 * D + 16, :].astype(F32)
    transition = decode(ref[0:D, :], tile[0:1]) + jnp.where(eye, tile[2:3], 0.0)
    return transition, decode(ref[D:2 * D, :], tile[1:2])


def unit_lower_inverse(lower, rows, cols):
    def off_diagonal(size):
        place = (rows // (2 * size) == cols // (2 * size)) & (
            rows % (2 * size) >= size) & (cols % (2 * size) < size)
        return jnp.where(place, lower, 0.0)

    inverse = jnp.where(rows == cols, 1.0, 0.0) - off_diagonal(1)
    size = 2
    while size < L:
        inverse = inverse - mm3(mm3(inverse, off_diagonal(size), NN), inverse, NN)
        size *= 2
    return inverse


def block_front(k, v, beta_row, log_row, rows, cols):
    eye = rows == cols
    lower = rows >= cols

    def as_column(row):
        return row_sum(jnp.where(eye, row, 0.0))

    def as_row(column):
        return column_sum(jnp.where(eye, column, 0.0))

    beta = as_column(beta_row)
    total = row_sum(jnp.where(lower, log_row, 0.0))
    total_row = column_sum(jnp.where(rows <= cols, as_column(log_row), 0.0))
    decays = jnp.exp(jnp.where(lower, total - total_row, -1e30))
    last = total[L - 1:L, :]
    grown = jnp.exp(total)
    tail = jnp.exp(last - total)
    kf = k.astype(F32)
    rk = inverse_root(row_sum(kf * kf) + EPSILON)
    rk_row = as_row(rk)
    system = jnp.where(rows > cols, dot(k, k, NT) * (beta * rk) * (rk_row * decays), 0.0)
    inverse = unit_lower_inverse(system, rows, cols)
    fresh = mm2l(inverse * beta_row, v, NN)
    weights = mm2l(inverse * (beta_row * jnp.exp(total_row) * rk_row), k, NN)
    both = cat([weights, fresh], 1)
    moved = mm2l(both * (tail * rk), k, TN)
    transition = jnp.where(eye, jnp.exp(last), 0.0) - moved[:D]
    return dict(
        beta=beta, grown=grown, tail=tail, decays=decays, rk=rk, rk_row=rk_row, inverse=inverse,
        fresh=fresh, weights=weights, both=both, transition=transition, injection=moved[D:])


def block_reach(f, q, k, g):
    qf = q.astype(F32)
    rq = inverse_root(row_sum(qf * qf) + EPSILON)
    scores = dot(q, k, NT) * rq * (f["rk_row"] * f["decays"])
    seen = mm3(scores, f["both"], NN)
    reach = qf * (rq * f["grown"]) - seen[:, :D]
    return dict(
        rq=rq, inner=seen[:, D:], reach=reach, back=mm2l(scores, g, TN), adjoint=mm2r(g, reach, TN))


def block_back(f, q, k, v, g, state, later, leaving, rows, cols):
    qf, kf, vf, gf = q.astype(F32), k.astype(F32), v.astype(F32), g.astype(F32)
    through = mm3(cat([f["weights"], f["reach"]], 0), state, NT)
    corrected = f["fresh"] - through[:L]
    outputs = through[L:] + f["inner"]
    rk, rq, beta, decays = f["rk"], f["rq"], f["beta"], f["decays"]
    d_corrected = f["back"] + (f["tail"] * rk) * mm2r(k, later, NT)
    d_right = mm3(f["inverse"], d_corrected, TN)
    d_value = beta * d_right
    d_beta = row_sum(d_right * corrected) / beta
    flow = row_sum(gf * outputs) - row_sum(d_value * vf)
    d_scores = mm2r(g, corrected, NT) * decays
    d_system = jnp.where(rows > cols, mm3(d_right, corrected, NT) * (beta * decays), 0.0)
    d_q = f["grown"] * mm2r(g, state, NN) + mm2l(d_scores * f["rk_row"], k, NN)
    d_k = (mm2l(d_scores * rq, q, TN) + f["tail"] * mm3(corrected, later, NN)
           - mm3(d_value * f["grown"], state, NN)
           - mm2l(d_system * f["rk_row"], k, NN) - mm2l(d_system * rk, k, TN))

    def norm_back(unit, scale, grad):
        return scale * (grad - unit * row_sum(unit * grad))

    d_beta_row = column_sum(jnp.where(rows == cols, d_beta, 0.0))
    d_log_row = column_sum(jnp.where(rows >= cols, flow, 0.0)) + leaving
    return (outputs, norm_back(qf * rq, rq, d_q), norm_back(kf * rk, rk, d_k), d_value,
            d_beta_row, d_log_row)


def layer_kernel(cfg, q_hbm, k_hbm, v_hbm, g_hbm, beta_hbm, log_hbm,
                 out16, out_gates,
                 q_ref, k_ref, v_ref, g_ref, beta_ref, log_ref, pack_kv, pack_qg, landed_kv, landed_qg,
                 gate_pack, gate_landed, own, other, z_steps, z_back,
                 before, after, y_up, y_down, from_lower, from_upper, forward, backward,
                 hand, held, res16, gate_res,
                 load_sem, in_send, in_recv, core_send, core_recv,
                 z_send, z_recv, y_send, y_recv, out_send, out_recv):
    X, Q, J, Y = cfg
    heads, lanes = X * Q, 2 * X
    rows_dev = L // lanes
    nb = Q // 2
    slots = nb * lanes
    hd, sq = lax.axis_index("head"), lax.axis_index("seq")
    x, c = hd // 2, hd % 2
    y, z = sq // (J * Q), sq % (J * Q)
    j, i = z // Q, z % Q
    base = y * (J * Q) + j * Q
    at_home = i // nb == c
    scans = c == 0
    helps = c == 1
    partner = (x * 2 + 1 - c, sq)

    def remote(src, dst, send, recv, there):
        return pltpu.make_async_remote_copy(
            src_ref=src, dst_ref=dst, send_sem=send, recv_sem=recv, device_id=there, device_id_type=MESH)

    def await_bytes(ref, sem):
        pltpu.make_async_copy(ref, ref, sem).wait()

    def z_device(place):
        return (hd, y * (J * Q) + place * Q + i)

    def y_device(place):
        return (hd, place * (J * Q) + z)

    loads = [pltpu.make_async_copy(src, dst, load_sem.at[n]) for n, (src, dst) in enumerate((
        (k_hbm, k_ref), (v_hbm, v_ref), (beta_hbm, beta_ref), (log_hbm, log_ref),
        (q_hbm, q_ref), (g_hbm, g_ref)))]
    for load in loads:
        load.start()

    barrier = pltpu.get_barrier_semaphore()

    def greet_group(n, carry):
        there = (n // Q, base + n % Q)

        @pl.when((there[0] != hd) | (there[1] != sq))
        def _():
            pl.semaphore_signal(barrier, inc=1, device_id=there, device_id_type=MESH)
        return carry

    lax.fori_loop(0, lanes * Q, greet_group, 0)

    @pl.when(scans)
    def _():
        for step in range(1, J):
            pl.semaphore_signal(
                barrier, inc=1, device_id=z_device((j + step) % J), device_id_type=MESH)
        for step in range(1, Y):
            pl.semaphore_signal(
                barrier, inc=1, device_id=y_device((y + step) % Y), device_id_type=MESH)

    for load in loads:
        load.wait()
    for h in range(heads):
        for pack, refs in ((pack_kv, (k_ref, v_ref)), (pack_qg, (q_ref, g_ref))):
            for n, ref in enumerate(refs):
                pack[h, n * rows_dev:(n + 1) * rows_dev, :] = ref[0, :, h * D:(h + 1) * D]
    for r in range(nb):
        gate_pack[r, 0:1, :] = beta_ref[r:r + 1, :]
        gate_pack[r, 1:2, :] = log_ref[r:r + 1, :]

    @pl.when(scans)
    def _():
        pl.semaphore_wait(barrier, lanes * Q - 1 + J - 1 + Y - 1)

    @pl.when(helps)
    def _():
        pl.semaphore_wait(barrier, lanes * Q - 1)

    own_head = x * Q + i
    own_slot = (i % nb) * lanes + hd

    def send_rows_in(pack, landed, n):
        def send(m, carry):
            there_x, there_i = x ^ (X - 1 - m % X), i ^ (Q - 1 - m // X)

            @pl.when((m != heads - 1) | jnp.logical_not(at_home))
            def _():
                remote(pack.at[there_x * Q + there_i], landed.at[own_slot], in_send.at[n],
                       in_recv.at[n], (there_x * 2 + i // nb, base + there_i)).start()
            return carry

        lax.fori_loop(0, heads, send, 0)

        @pl.when(at_home)
        def _():
            landed[own_slot] = pack[own_head]

    for r in range(nb):
        there = (x * 2 + i // nb, base + nb * c + r)
        here = at_home & (i % nb == r)

        @pl.when(jnp.logical_not(here))
        def _():
            remote(gate_pack.at[r], gate_landed.at[i % nb], in_send.at[2], in_recv.at[2], there).start()

        @pl.when(here)
        def _():
            gate_landed[i % nb] = gate_pack[r]

    send_rows_in(pack_kv, landed_kv, 0)
    send_rows_in(pack_qg, landed_qg, 1)

    def settle(ref, count, sem):
        @pl.when(at_home)
        def _():
            await_bytes(ref.at[pl.ds(0, count - 1)], sem)

        @pl.when(jnp.logical_not(at_home))
        def _():
            await_bytes(ref.at[pl.ds(0, count)], sem)

    rows = lax.broadcasted_iota(jnp.int32, (L, L), 0)
    cols = lax.broadcasted_iota(jnp.int32, (L, L), 1)
    eye = rows == cols

    def operands(b, landed):
        part_ = landed.at[b * lanes:(b + 1) * lanes]
        return [part_[:, n * rows_dev:(n + 1) * rows_dev, :].reshape(L, D) for n in range(2)]

    settle(gate_landed, nb, in_recv.at[2])
    settle(landed_kv, slots, in_recv.at[0])
    blocks = []
    for b in range(nb):
        k, v = operands(b, landed_kv)
        blocks.append(block_front(k, v, gate_landed[b, 0:1, :], gate_landed[b, 1:2, :], rows, cols))
    first, second = blocks
    joined = mm3(cat([first["transition"], first["injection"]], 0), second["transition"], NN)
    own[0] = joined[:D]
    own[1] = joined[D:] + second["injection"]

    @pl.when(helps)
    def _():
        remote(own.at[pl.ds(0, 2)], other.at[pl.ds(0, 2)], core_send.at[0], core_recv.at[0], partner).start()

    settle(landed_qg, slots, in_recv.at[1])

    def reach(b):
        q, g = operands(b, landed_qg)
        blocks[b].update(block_reach(blocks[b], q, operands(b, landed_kv)[0], g))

    reach(0)

    @pl.when(scans)
    def _():
        await_bytes(other.at[pl.ds(0, 2)], core_recv.at[0])
        chip = mm3(cat([own[0], own[1]], 0), other[0], NN)
        put_step(z_steps.at[j], encode_transition(chip[:D], eye), chip[D:] + other[1])
        for step in range(1, J):
            remote(z_steps.at[j], z_steps.at[j], z_send.at[0, step - 1], z_recv.at[0, step - 1],
                   z_device((j + step) % J)).start()

    reach(1)
    own[2] = mm3(second["adjoint"], first["transition"], NT) + first["adjoint"]

    @pl.when(helps)
    def _():
        remote(own.at[2], other.at[2], core_send.at[1], core_recv.at[1], partner).start()

    @pl.when(scans)
    def _():
        await_bytes(other.at[2], core_recv.at[1])
        code, scale = encode(mm3(other[2], own[0], NT) + own[2])
        z_back[j, 0:D, :] = code
        z_back[j, D:, :] = scale_rows([scale])
        for step in range(1, J):
            remote(z_back.at[j], z_back.at[j], z_send.at[1, step - 1], z_recv.at[1, step - 1],
                   z_device((j + step) % J)).start()
        for step in range(1, J):
            await_bytes(z_steps.at[0], z_recv.at[0, step - 1])
        steps = [decode_step(z_steps.at[m], eye) for m in range(J)]
        one = jnp.where(eye, 1.0, 0.0)
        before[0] = cat([one, jnp.zeros((D, D), F32)], 0)
        run = cat(steps[0], 0)
        for m in range(1, J):
            before[m] = run
            run = mm3(run, steps[m][0], NN)
            run = cat([run[:D], run[D:] + steps[m][1]], 0)
        row_transition = encode_transition(run[:D], eye)
        put_step(y_up, row_transition, run[D:])
        for step in range(1, J):
            await_bytes(z_back.at[0], z_recv.at[1, step - 1])
        shifts = [decode(z_back[m, 0:D, :], z_back[m, D:, :].astype(F32)[0:1]) for m in range(J)]
        after[J - 1] = cat([one, jnp.zeros((D, D), F32)], 0)
        run = cat([steps[J - 1][0].T, shifts[J - 1]], 0)
        for m in range(J - 2, -1, -1):
            after[m] = run
            run = mm3(run, steps[m][0], NT)
            run = cat([run[:D], run[D:] + shifts[m]], 0)
        put_step(y_down, row_transition, run[D:])

        for step in range(1, Y):
            place = (y + step) % Y

            @pl.when(place > y)
            def _():
                remote(y_up, from_lower.at[y], y_send.at[step - 1], y_recv.at[step - 1],
                       y_device(place)).start()

            @pl.when(place < y)
            def _():
                remote(y_down, from_upper.at[y], y_send.at[step - 1], y_recv.at[step - 1],
                       y_device(place)).start()
        for step in range(1, Y):
            await_bytes(from_lower.at[0], y_recv.at[step - 1])
        forward[...] = jnp.zeros((D, D), F32)
        backward[...] = jnp.zeros((D, D), F32)
        for m in range(Y - 1):
            @pl.when(m < y)
            def _():
                step_t, step_s = decode_step(from_lower.at[m], eye)
                forward[...] = mm3(forward[...], step_t, NN) + step_s

            @pl.when(Y - 1 - m > y)
            def _():
                step_t, step_s = decode_step(from_upper.at[Y - 1 - m], eye)
                backward[...] = mm3(backward[...], step_t, NT) + step_s

        hand[0] = mm3(backward[...], after[j, 0:D, :], NN) + after[j, D:, :]
        remote(hand.at[0], held.at[0], core_send.at[0], core_recv.at[0], partner).start()
        held[1] = mm3(forward[...], before[j, 0:D, :], NN) + before[j, D:, :]
        hand[1] = mm3(held[1], own[0], NN) + own[1]
        remote(hand.at[1], held.at[1], core_send.at[1], core_recv.at[1], partner).start()
        held[0] = mm3(hand[0], other[0], NT) + other[2]

    @pl.when(helps)
    def _():
        await_bytes(held.at[0], core_recv.at[0])
        await_bytes(held.at[1], core_recv.at[1])

    later, state = held[0], held[1]

    middle_state = mm3(state, first["transition"], NN) + first["injection"]
    middle_later = mm3(later, second["transition"], NT) + second["adjoint"]

    def inner(m, n):
        return column_sum(row_sum(m * n))

    leaving = (inner(middle_later, middle_state),
               inner(middle_later - second["adjoint"], middle_state) + inner(later, second["injection"]))
    for b, (f, s, n) in enumerate(((first, state, middle_later), (second, middle_state, later))):
        k, v = operands(b, landed_kv)
        q, g = operands(b, landed_qg)
        outputs, d_q, d_k, d_v, d_beta, d_log = block_back(f, q, k, v, g, s, n, leaving[b], rows, cols)
        message = res16.at[b * lanes:(b + 1) * lanes]
        message[:, 0:rows_dev, :] = outputs.astype(BF16).reshape(lanes, rows_dev, D)
        scales = []
        for n_, grad in enumerate((d_q, d_k, d_v)):
            code, scale = encode(grad.reshape(lanes, rows_dev, D), 1)
            message[:, (n_ + 1) * rows_dev:(n_ + 2) * rows_dev, :] = code
            scales.append(scale)
        message[:, 4 * rows_dev:, :] = scale_rows(scales)
        gate_res[b, 0:1, :] = d_beta
        gate_res[b, 1:2, :] = d_log

    def send_rows_back(m, carry):
        slot = own_slot ^ (slots - 1 - m)
        there = (slot % lanes, base + nb * c + slot // lanes)

        @pl.when((m != slots - 1) | jnp.logical_not(at_home))
        def _():
            remote(res16.at[slot], out16.at[own_head], out_send.at[0], out_recv.at[0], there).start()
        return carry

    lax.fori_loop(0, slots, send_rows_back, 0)
    for m in range(nb):
        there = (x * 2 + i // nb, base + nb * c + m)
        here = at_home & (i % nb == m)

        @pl.when(jnp.logical_not(here))
        def _():
            remote(gate_res.at[m], out_gates.at[i % nb], out_send.at[1], out_recv.at[1], there).start()

        @pl.when(here)
        def _():
            out_gates[i % nb] = gate_res[m]

    @pl.when(at_home)
    def _():
        out16[own_head] = res16[own_slot]

    settle(pack_kv, heads, in_send.at[0])
    settle(pack_qg, heads, in_send.at[1])
    settle(gate_pack, nb, in_send.at[2])

    @pl.when(helps)
    def _():
        await_bytes(own.at[pl.ds(0, 2)], core_send.at[0])
        await_bytes(own.at[2], core_send.at[1])

    @pl.when(scans)
    def _():
        await_bytes(hand.at[0], core_send.at[0])
        await_bytes(hand.at[1], core_send.at[1])
        for step in range(1, J):
            await_bytes(z_steps.at[0], z_send.at[0, step - 1])
            await_bytes(z_back.at[0], z_send.at[1, step - 1])
        for step in range(1, Y):
            await_bytes(y_up, y_send.at[step - 1])

    settle(out_gates, nb, out_recv.at[1])
    settle(out16, heads, out_recv.at[0])
    settle(res16, slots, out_send.at[0])
    settle(gate_res, nb, out_send.at[1])


def unpack_kernel(in16_hbm, gates_hbm, att, d_q, d_k, d_v, d_beta, d_log,
                  in16, in_gates, wide16, wide32, gates, in_sems, sems):
    heads = in16.shape[0]
    rows_dev = wide16.shape[0]
    loads = [pltpu.make_async_copy(in16_hbm, in16, in_sems.at[0]),
             pltpu.make_async_copy(gates_hbm, in_gates, in_sems.at[1])]
    for load in loads:
        load.start()
    for load in loads:
        load.wait()
    copies = []
    for n, out in enumerate((d_q, d_k, d_v)):
        for h in range(heads):
            scales = in16[h, 4 * rows_dev:4 * rows_dev + 16, :].astype(F32)
            wide32[n, :, h * D:(h + 1) * D] = decode(
                in16[h, (n + 1) * rows_dev:(n + 2) * rows_dev, :], scales[n:n + 1])
        copies.append(pltpu.make_async_copy(wide32.at[n], out.at[0], sems.at[n]))
        copies[-1].start()
    for h in range(heads):
        wide16[:, h * D:(h + 1) * D] = in16[h, 0:rows_dev, :]
    copies.append(pltpu.make_async_copy(wide16, att.at[0], sems.at[3]))
    copies[-1].start()
    for n, out in enumerate((d_beta, d_log)):
        for r in range(in_gates.shape[0]):
            gates[n, r:r + 1, :] = in_gates[r, n:n + 1, :]
        copies.append(pltpu.make_async_copy(gates.at[n], out, sems.at[4 + n]))
        copies[-1].start()
    for copy in copies:
        copy.wait()


def shards(cfg, queries, key_inputs, values, beta_gates, log_decay, out_grad):
    X, Q, J, Y = cfg
    heads, lanes = X * Q, 2 * X
    rows_dev = L // lanes
    nb = Q // 2
    slots = nb * lanes
    vmem = pl.BlockSpec(memory_space=pltpu.VMEM)
    hbm = pl.BlockSpec(memory_space=pl.ANY)
    dma = pltpu.SemaphoreType.DMA

    def wide(shape, kind=F32):
        return pltpu.VMEM(shape, kind)

    landed = pl.pallas_call(
        functools.partial(layer_kernel, cfg),
        out_shape=(
            jax.ShapeDtypeStruct((heads, 4 * rows_dev + 16, D), BF16),
            jax.ShapeDtypeStruct((nb, 8, L), F32),
        ),
        in_specs=[hbm] * 6,
        out_specs=(vmem, vmem),
        scratch_shapes=[
            *[wide((1, rows_dev, heads * D), BF16)] * 4, wide((nb, L)), wide((nb, L)),
            *[wide((heads, 2 * rows_dev, D), BF16)] * 2, *[wide((slots, 2 * rows_dev, D), BF16)] * 2,
            wide((nb, 8, L)), wide((nb, 8, L)), wide((3, D, D)), wide((3, D, D)),
            wide((J, 2 * D + 16, D), BF16), wide((J, D + 16, D), BF16),
            *[wide((J, 2 * D, D))] * 2, *[wide((2 * D + 16, D), BF16)] * 2,
            *[wide((Y, 2 * D + 16, D), BF16)] * 2, *[wide((D, D))] * 2, wide((2, D, D)), wide((2, D, D)),
            wide((slots, 4 * rows_dev + 16, D), BF16), wide((nb, 8, L)),
            dma((6,)), dma((3,)), dma((3,)), dma((2,)), dma((2,)),
            dma((2, J - 1)), dma((2, J - 1)), dma((Y - 1,)), dma((Y - 1,)), dma((2,)), dma((2,)),
        ],
        compiler_params=pltpu.CompilerParams(
            collective_id=0, has_side_effects=True, vmem_limit_bytes=56 * 1024 * 1024),
        name="delta_rule",
    )(queries, key_inputs, values, out_grad, beta_gates, log_decay)
    rows = jax.ShapeDtypeStruct((1, rows_dev, heads * D), F32)
    gates = jax.ShapeDtypeStruct((nb, L), F32)
    return pl.pallas_call(
        unpack_kernel,
        out_shape=(jax.ShapeDtypeStruct(rows.shape, BF16), rows, rows, rows, gates, gates),
        in_specs=[hbm] * 2,
        out_specs=(hbm,) * 6,
        scratch_shapes=[
            wide((heads, 4 * rows_dev + 16, D), BF16), wide((nb, 8, L)),
            wide((rows_dev, heads * D), BF16), wide((3, rows_dev, heads * D)), wide((2, nb, L)),
            dma((2,)), dma((6,))],
        compiler_params=pltpu.CompilerParams(vmem_limit_bytes=56 * 1024 * 1024),
        name="unpack",
    )(*landed)


def build(mesh, y_chips):
    X = mesh.shape["head"] // 2
    heads = 16 if y_chips == 4 else 4 * X
    Q = heads // X
    J = mesh.shape["seq"] // (y_chips * Q)
    rows = P("seq", "head", None)
    gates = P("head", "seq")
    return jax.shard_map(
        functools.partial(shards, (X, Q, J, y_chips)), mesh=mesh,
        in_specs=(rows, rows, rows, gates, gates, rows),
        out_specs=(rows, rows, rows, rows, gates, gates), check_vma=False)


def solution(mesh):
    return build(mesh, 4)
```

```python
import functools
import math

import jax
import jax.numpy as jnp
from jax import lax
from jax.experimental import pallas as pl
from jax.experimental.pallas import tpu as pltpu
from jax.sharding import PartitionSpec as P

D = 128
L = 128
EPSILON = 1e-06
SPAN = 240.0
F32, BF16 = jnp.float32, jnp.bfloat16
MESH = pl.DeviceIdType.MESH
NN = (((1,), (0,)), ((), ()))
NT = (((1,), (1,)), ((), ()))
TN = (((0,), (0,)), ((), ()))


def split(x):
    high = x.astype(BF16)
    return high, (x - high.astype(F32)).astype(BF16)


def dot(a, b, dims):
    return lax.dot_general(a, b, dims, preferred_element_type=F32)


def cat(parts, dim):
    return jnp.concatenate(parts, axis=dim)


def mm3(a, b, dims):
    ah, al = split(a)
    bh, bl = split(b)
    ca, cb = dims[0][0][0], dims[0][1][0]
    return dot(cat([ah, al, ah], ca), cat([bh, bh, bl], cb), dims)


def mm2l(a, b, dims):
    ah, al = split(a)
    ca, cb = dims[0][0][0], dims[0][1][0]
    return dot(cat([ah, al], ca), cat([b, b], cb), dims)


def mm2r(a, b, dims):
    bh, bl = split(b)
    ca, cb = dims[0][0][0], dims[0][1][0]
    return dot(cat([a, a], ca), cat([bh, bl], cb), dims)


def inverse_root(total):
    guess = lax.rsqrt(total)
    return guess * (1.5 - 0.5 * total * guess * guess)


def row_sum(x):
    return jnp.sum(x, axis=1, keepdims=True)


def column_sum(x):
    return jnp.sum(x, axis=0, keepdims=True)


def encode(values, dim=0):
    scale = (jnp.maximum(jnp.max(jnp.abs(values), axis=dim, keepdims=True), 1e-30) * 1.01).astype(BF16)
    scale = scale.astype(F32)
    code = jnp.exp2(jnp.abs(values) * (SPAN / scale) - SPAN / 2)
    return jnp.where(values < 0, -code, code).astype(BF16), scale


def decode(code, scale):
    code = code.astype(F32)
    size = (jnp.log(jnp.abs(code)) * (1 / math.log(2)) + SPAN / 2) * (scale / SPAN)
    return jnp.where(code < 0, -size, size)


def scale_rows(scales):
    shape = scales[0].shape[:-2] + (16, D)
    row = lax.broadcasted_iota(jnp.int32, shape, len(shape) - 2)
    tile = jnp.zeros(shape, F32)
    for n, scale in enumerate(scales):
        tile = jnp.where(row == n, scale, tile)
    return tile.astype(BF16)


def encode_transition(transition, eye):
    diagonal = column_sum(row_sum(jnp.where(eye, transition, 0.0))) / D
    diagonal = diagonal.astype(BF16).astype(F32)
    code, scale = encode(transition - jnp.where(eye, diagonal, 0.0))
    return code, scale, diagonal


def put_step(ref, coded_transition, shift):
    code, scale, diagonal = coded_transition
    ref[0:D, :] = code
    code, shift_scale = encode(shift)
    ref[D:2 * D, :] = code
    ref[2 * D:2 * D + 16, :] = scale_rows([scale, shift_scale, diagonal])


def decode_step(ref, eye):
    tile = ref[2 * D:2 * D + 16, :].astype(F32)
    transition = decode(ref[0:D, :], tile[0:1]) + jnp.where(eye, tile[2:3], 0.0)
    return transition, decode(ref[D:2 * D, :], tile[1:2])


def unit_lower_inverse(lower, rows, cols):
    def off_diagonal(size):
        place = (rows // (2 * size) == cols // (2 * size)) & (
            rows % (2 * size) >= size) & (cols % (2 * size) < size)
        return jnp.where(place, lower, 0.0)

    inverse = jnp.where(rows == cols, 1.0, 0.0) - off_diagonal(1)
    size = 2
    while size < L:
        inverse = inverse - mm3(mm3(inverse, off_diagonal(size), NN), inverse, NN)
        size *= 2
    return inverse


def block_front(k, v, beta_row, log_row, rows, cols):
    eye = rows == cols
    lower = rows >= cols

    def as_column(row):
        return row_sum(jnp.where(eye, row, 0.0))

    def as_row(column):
        return column_sum(jnp.where(eye, column, 0.0))

    beta = as_column(beta_row)
    total = row_sum(jnp.where(lower, log_row, 0.0))
    total_row = column_sum(jnp.where(rows <= cols, as_column(log_row), 0.0))
    decays = jnp.exp(jnp.where(lower, total - total_row, -1e30))
    last = total[L - 1:L, :]
    grown = jnp.exp(total)
    tail = jnp.exp(last - total)
    kf = k.astype(F32)
    rk = inverse_root(row_sum(kf * kf) + EPSILON)
    rk_row = as_row(rk)
    system = jnp.where(rows > cols, dot(k, k, NT) * (beta * rk) * (rk_row * decays), 0.0)
    inverse = unit_lower_inverse(system, rows, cols)
    fresh = mm2l(inverse * beta_row, v, NN)
    weights = mm2l(inverse * (beta_row * jnp.exp(total_row) * rk_row), k, NN)
    both = cat([weights, fresh], 1)
    moved = mm2l(both * (tail * rk), k, TN)
    transition = jnp.where(eye, jnp.exp(last), 0.0) - moved[:D]
    return dict(
        beta=beta, grown=grown, tail=tail, decays=decays, rk=rk, rk_row=rk_row, inverse=inverse,
        fresh=fresh, weights=weights, both=both, transition=transition, injection=moved[D:])


def block_reach(f, q, k, g):
    qf = q.astype(F32)
    rq = inverse_root(row_sum(qf * qf) + EPSILON)
    scores = dot(q, k, NT) * rq * (f["rk_row"] * f["decays"])
    seen = mm3(scores, f["both"], NN)
    reach = qf * (rq * f["grown"]) - seen[:, :D]
    return dict(
        rq=rq, inner=seen[:, D:], reach=reach, back=mm2l(scores, g, TN), adjoint=mm2r(g, reach, TN))


def block_back(f, q, k, v, g, state, later, leaving, rows, cols):
    qf, kf, vf, gf = q.astype(F32), k.astype(F32), v.astype(F32), g.astype(F32)
    through = mm3(cat([f["weights"], f["reach"]], 0), state, NT)
    corrected = f["fresh"] - through[:L]
    outputs = through[L:] + f["inner"]
    rk, rq, beta, decays = f["rk"], f["rq"], f["beta"], f["decays"]
    d_corrected = f["back"] + (f["tail"] * rk) * mm2r(k, later, NT)
    d_right = mm3(f["inverse"], d_corrected, TN)
    d_value = beta * d_right
    d_beta = row_sum(d_right * corrected) / beta
    flow = row_sum(gf * outputs) - row_sum(d_value * vf)
    d_scores = mm2r(g, corrected, NT) * decays
    d_system = jnp.where(rows > cols, mm3(d_right, corrected, NT) * (beta * decays), 0.0)
    d_q = f["grown"] * mm2r(g, state, NN) + mm2l(d_scores * f["rk_row"], k, NN)
    d_k = (mm2l(d_scores * rq, q, TN) + f["tail"] * mm3(corrected, later, NN)
           - mm3(d_value * f["grown"], state, NN)
           - mm2l(d_system * f["rk_row"], k, NN) - mm2l(d_system * rk, k, TN))

    def norm_back(unit, scale, grad):
        return scale * (grad - unit * row_sum(unit * grad))

    d_beta_row = column_sum(jnp.where(rows == cols, d_beta, 0.0))
    d_log_row = column_sum(jnp.where(rows >= cols, flow, 0.0)) + leaving
    return (outputs, norm_back(qf * rq, rq, d_q), norm_back(kf * rk, rk, d_k), d_value,
            d_beta_row, d_log_row)


def layer_kernel(cfg, q_hbm, k_hbm, v_hbm, g_hbm, beta_hbm, log_hbm,
                 out16, out_gates,
                 q_ref, k_ref, v_ref, g_ref, beta_ref, log_ref, pack_kv, pack_qg, landed_kv, landed_qg,
                 gate_pack, gate_landed, own, other, z_steps, z_back,
                 before, after, core_before, core_after, y_up, y_down, from_lower, from_upper, forward, backward,
                 hand, held, res16, gate_res,
                 load_sem, in_send, in_recv, core_send, core_recv,
                 z_send, z_recv, y_send, y_recv, out_send, out_recv):
    X, Q, J, Y = cfg
    heads, lanes = X * Q, 2 * X
    rows_dev = L // lanes
    nb = Q // 2
    slots = nb * lanes
    hd, sq = lax.axis_index("head"), lax.axis_index("seq")
    x, c = hd // 2, hd % 2
    y, z = sq // (J * Q), sq % (J * Q)
    j, i = z // Q, z % Q
    base = y * (J * Q) + j * Q
    at_home = i // nb == c
    scans = c == 0
    helps = c == 1
    partner = (x * 2 + 1 - c, sq)

    def remote(src, dst, send, recv, there):
        return pltpu.make_async_remote_copy(
            src_ref=src, dst_ref=dst, send_sem=send, recv_sem=recv, device_id=there, device_id_type=MESH)

    def await_bytes(ref, sem):
        pltpu.make_async_copy(ref, ref, sem).wait()

    def farthest(ring):
        return sorted(range(1, ring), key=lambda step: -min(step, ring - step))

    def z_device(place):
        return (hd, y * (J * Q) + place * Q + i)

    def y_device(place):
        return (hd, place * (J * Q) + z)

    loads = [pltpu.make_async_copy(src, dst, load_sem.at[n]) for n, (src, dst) in enumerate((
        (k_hbm, k_ref), (v_hbm, v_ref), (beta_hbm, beta_ref), (log_hbm, log_ref),
        (q_hbm, q_ref), (g_hbm, g_ref)))]
    for load in loads:
        load.start()

    barrier = pltpu.get_barrier_semaphore()

    def greet_group(n, carry):
        there = (n // Q, base + n % Q)

        @pl.when((there[0] != hd) | (there[1] != sq))
        def _():
            pl.semaphore_signal(barrier, inc=1, device_id=there, device_id_type=MESH)
        return carry

    lax.fori_loop(0, lanes * Q, greet_group, 0)

    @pl.when(scans)
    def _():
        for step in range(1, J):
            pl.semaphore_signal(
                barrier, inc=1, device_id=z_device((j + step) % J), device_id_type=MESH)
        for step in range(1, Y):
            pl.semaphore_signal(
                barrier, inc=1, device_id=y_device((y + step) % Y), device_id_type=MESH)

    for load in loads:
        load.wait()
    for h in range(heads):
        for pack, refs in ((pack_kv, (k_ref, v_ref)), (pack_qg, (q_ref, g_ref))):
            for n, ref in enumerate(refs):
                pack[h, n * rows_dev:(n + 1) * rows_dev, :] = ref[0, :, h * D:(h + 1) * D]
    for r in range(nb):
        gate_pack[r, 0:1, :] = beta_ref[r:r + 1, :]
        gate_pack[r, 1:2, :] = log_ref[r:r + 1, :]

    @pl.when(scans)
    def _():
        pl.semaphore_wait(barrier, lanes * Q - 1 + J - 1 + Y - 1)

    @pl.when(helps)
    def _():
        pl.semaphore_wait(barrier, lanes * Q - 1)

    own_head = x * Q + i
    own_slot = (i % nb) * lanes + hd

    def send_rows_in(pack, landed, n):
        def send(m, carry):
            there_x, there_i = x ^ (X - 1 - m % X), i ^ (Q - 1 - m // X)

            @pl.when((m != heads - 1) | jnp.logical_not(at_home))
            def _():
                remote(pack.at[there_x * Q + there_i], landed.at[own_slot], in_send.at[n],
                       in_recv.at[n], (there_x * 2 + i // nb, base + there_i)).start()
            return carry

        lax.fori_loop(0, heads, send, 0)

        @pl.when(at_home)
        def _():
            landed[own_slot] = pack[own_head]

    for r in range(nb):
        there = (x * 2 + i // nb, base + nb * c + r)
        here = at_home & (i % nb == r)

        @pl.when(jnp.logical_not(here))
        def _():
            remote(gate_pack.at[r], gate_landed.at[i % nb], in_send.at[2], in_recv.at[2], there).start()

        @pl.when(here)
        def _():
            gate_landed[i % nb] = gate_pack[r]

    send_rows_in(pack_kv, landed_kv, 0)
    send_rows_in(pack_qg, landed_qg, 1)

    def settle(ref, count, sem):
        @pl.when(at_home)
        def _():
            await_bytes(ref.at[pl.ds(0, count - 1)], sem)

        @pl.when(jnp.logical_not(at_home))
        def _():
            await_bytes(ref.at[pl.ds(0, count)], sem)

    rows = lax.broadcasted_iota(jnp.int32, (L, L), 0)
    cols = lax.broadcasted_iota(jnp.int32, (L, L), 1)
    eye = rows == cols

    def operands(b, landed):
        part_ = landed.at[b * lanes:(b + 1) * lanes]
        return [part_[:, n * rows_dev:(n + 1) * rows_dev, :].reshape(L, D) for n in range(2)]

    settle(gate_landed, nb, in_recv.at[2])
    settle(landed_kv, slots, in_recv.at[0])
    blocks = []
    for b in range(nb):
        k, v = operands(b, landed_kv)
        blocks.append(block_front(k, v, gate_landed[b, 0:1, :], gate_landed[b, 1:2, :], rows, cols))
    first, second = blocks
    joined = mm3(cat([first["transition"], first["injection"]], 0), second["transition"], NN)
    own[0] = joined[:D]
    own[1] = joined[D:] + second["injection"]

    @pl.when(helps)
    def _():
        remote(own.at[pl.ds(0, 2)], other.at[pl.ds(0, 2)], core_send.at[0], core_recv.at[0], partner).start()

    settle(landed_qg, slots, in_recv.at[1])

    def reach(b):
        q, g = operands(b, landed_qg)
        blocks[b].update(block_reach(blocks[b], q, operands(b, landed_kv)[0], g))

    reach(0)

    @pl.when(scans)
    def _():
        await_bytes(other.at[pl.ds(0, 2)], core_recv.at[0])
        chip = mm3(cat([own[0], own[1]], 0), other[0], NN)
        put_step(z_steps.at[j], encode_transition(chip[:D], eye), chip[D:] + other[1])
        for step in farthest(J):
            remote(z_steps.at[j], z_steps.at[j], z_send.at[0, step - 1], z_recv.at[0, step - 1],
                   z_device((j + step) % J)).start()

    reach(1)
    own[2] = mm3(second["adjoint"], first["transition"], NT) + first["adjoint"]

    @pl.when(helps)
    def _():
        remote(own.at[2], other.at[2], core_send.at[1], core_recv.at[1], partner).start()

    @pl.when(scans)
    def _():
        await_bytes(other.at[2], core_recv.at[1])
        code, scale = encode(mm3(other[2], own[0], NT) + own[2])
        z_back[j, 0:D, :] = code
        z_back[j, D:, :] = scale_rows([scale])
        for step in farthest(J):
            remote(z_back.at[j], z_back.at[j], z_send.at[1, step - 1], z_recv.at[1, step - 1],
                   z_device((j + step) % J)).start()
        for step in range(1, J):
            await_bytes(z_steps.at[0], z_recv.at[0, step - 1])
        steps = [decode_step(z_steps.at[m], eye) for m in range(J)]
        one = jnp.where(eye, 1.0, 0.0)
        before[0] = cat([one, jnp.zeros((D, D), F32)], 0)
        run = cat(steps[0], 0)
        for m in range(1, J):
            before[m] = run
            run = mm3(run, steps[m][0], NN)
            run = cat([run[:D], run[D:] + steps[m][1]], 0)
        row_transition = encode_transition(run[:D], eye)
        put_step(y_up, row_transition, run[D:])
        for step in range(1, J):
            await_bytes(z_back.at[0], z_recv.at[1, step - 1])
        shifts = [decode(z_back[m, 0:D, :], z_back[m, D:, :].astype(F32)[0:1]) for m in range(J)]
        after[J - 1] = cat([one, jnp.zeros((D, D), F32)], 0)
        run = cat([steps[J - 1][0].T, shifts[J - 1]], 0)
        for m in range(J - 2, -1, -1):
            after[m] = run
            run = mm3(run, steps[m][0], NT)
            run = cat([run[:D], run[D:] + shifts[m]], 0)
        put_step(y_down, row_transition, run[D:])

        for step in farthest(Y):
            place = (y + step) % Y

            @pl.when(place > y)
            def _():
                remote(y_up, from_lower.at[y], y_send.at[step - 1], y_recv.at[step - 1],
                       y_device(place)).start()

            @pl.when(place < y)
            def _():
                remote(y_down, from_upper.at[y], y_send.at[step - 1], y_recv.at[step - 1],
                       y_device(place)).start()
        run = mm3(before[j], own[0], NN)
        core_before[0] = run[:D]
        core_before[1] = run[D:] + own[1]
        run = mm3(after[j], other[0], NT)
        core_after[0] = run[:D]
        core_after[1] = run[D:] + other[2]
        for step in range(1, Y):
            await_bytes(from_lower.at[0], y_recv.at[step - 1])
        forward[...] = jnp.zeros((D, D), F32)
        backward[...] = jnp.zeros((D, D), F32)
        for m in range(Y - 1):
            @pl.when(m < y)
            def _():
                step_t, step_s = decode_step(from_lower.at[m], eye)
                forward[...] = mm3(forward[...], step_t, NN) + step_s

            @pl.when(Y - 1 - m > y)
            def _():
                step_t, step_s = decode_step(from_upper.at[Y - 1 - m], eye)
                backward[...] = mm3(backward[...], step_t, NT) + step_s

        down = mm3(backward[...], cat([after[j, 0:D, :], core_after[0]], 1), NN)
        up = mm3(forward[...], cat([before[j, 0:D, :], core_before[0]], 1), NN)
        hand[0] = down[:, :D] + after[j, D:, :]
        remote(hand.at[0], held.at[0], core_send.at[0], core_recv.at[0], partner).start()
        hand[1] = up[:, D:] + core_before[1]
        remote(hand.at[1], held.at[1], core_send.at[1], core_recv.at[1], partner).start()
        held[1] = up[:, :D] + before[j, D:, :]
        held[0] = down[:, D:] + core_after[1]

    @pl.when(helps)
    def _():
        await_bytes(held.at[0], core_recv.at[0])
        await_bytes(held.at[1], core_recv.at[1])

    later, state = held[0], held[1]

    middle_state = mm3(state, first["transition"], NN) + first["injection"]
    middle_later = mm3(later, second["transition"], NT) + second["adjoint"]

    def inner(m, n):
        return column_sum(row_sum(m * n))

    leaving = (inner(middle_later, middle_state),
               inner(middle_later - second["adjoint"], middle_state) + inner(later, second["injection"]))
    for b, (f, s, n) in enumerate(((first, state, middle_later), (second, middle_state, later))):
        k, v = operands(b, landed_kv)
        q, g = operands(b, landed_qg)
        outputs, d_q, d_k, d_v, d_beta, d_log = block_back(f, q, k, v, g, s, n, leaving[b], rows, cols)
        message = res16.at[b * lanes:(b + 1) * lanes]
        message[:, 0:rows_dev, :] = outputs.astype(BF16).reshape(lanes, rows_dev, D)
        scales = []
        for n_, grad in enumerate((d_q, d_k, d_v)):
            code, scale = encode(grad.reshape(lanes, rows_dev, D), 1)
            message[:, (n_ + 1) * rows_dev:(n_ + 2) * rows_dev, :] = code
            scales.append(scale)
        message[:, 4 * rows_dev:, :] = scale_rows(scales)
        gate_res[b, 0:1, :] = d_beta
        gate_res[b, 1:2, :] = d_log

    def send_rows_back(m, carry):
        slot = own_slot ^ (slots - 1 - m)
        there = (slot % lanes, base + nb * c + slot // lanes)

        @pl.when((m != slots - 1) | jnp.logical_not(at_home))
        def _():
            remote(res16.at[slot], out16.at[own_head], out_send.at[0], out_recv.at[0], there).start()
        return carry

    lax.fori_loop(0, slots, send_rows_back, 0)
    for m in range(nb):
        there = (x * 2 + i // nb, base + nb * c + m)
        here = at_home & (i % nb == m)

        @pl.when(jnp.logical_not(here))
        def _():
            remote(gate_res.at[m], out_gates.at[i % nb], out_send.at[1], out_recv.at[1], there).start()

        @pl.when(here)
        def _():
            out_gates[i % nb] = gate_res[m]

    @pl.when(at_home)
    def _():
        out16[own_head] = res16[own_slot]

    settle(pack_kv, heads, in_send.at[0])
    settle(pack_qg, heads, in_send.at[1])
    settle(gate_pack, nb, in_send.at[2])

    @pl.when(helps)
    def _():
        await_bytes(own.at[pl.ds(0, 2)], core_send.at[0])
        await_bytes(own.at[2], core_send.at[1])

    @pl.when(scans)
    def _():
        await_bytes(hand.at[0], core_send.at[0])
        await_bytes(hand.at[1], core_send.at[1])
        for step in range(1, J):
            await_bytes(z_steps.at[0], z_send.at[0, step - 1])
            await_bytes(z_back.at[0], z_send.at[1, step - 1])
        for step in range(1, Y):
            await_bytes(y_up, y_send.at[step - 1])

    settle(out_gates, nb, out_recv.at[1])
    settle(out16, heads, out_recv.at[0])
    settle(res16, slots, out_send.at[0])
    settle(gate_res, nb, out_send.at[1])


def unpack_kernel(in16_hbm, gates_hbm, att, d_q, d_k, d_v, d_beta, d_log,
                  in16, in_gates, wide16, wide32, gates, in_sems, sems):
    heads = in16.shape[0]
    rows_dev = wide16.shape[0]
    loads = [pltpu.make_async_copy(in16_hbm, in16, in_sems.at[0]),
             pltpu.make_async_copy(gates_hbm, in_gates, in_sems.at[1])]
    for load in loads:
        load.start()
    for load in loads:
        load.wait()
    copies = []
    for n, out in enumerate((d_q, d_k, d_v)):
        for h in range(heads):
            scales = in16[h, 4 * rows_dev:4 * rows_dev + 16, :].astype(F32)
            wide32[n, :, h * D:(h + 1) * D] = decode(
                in16[h, (n + 1) * rows_dev:(n + 2) * rows_dev, :], scales[n:n + 1])
        copies.append(pltpu.make_async_copy(wide32.at[n], out.at[0], sems.at[n]))
        copies[-1].start()
    for h in range(heads):
        wide16[:, h * D:(h + 1) * D] = in16[h, 0:rows_dev, :]
    copies.append(pltpu.make_async_copy(wide16, att.at[0], sems.at[3]))
    copies[-1].start()
    for n, out in enumerate((d_beta, d_log)):
        for r in range(in_gates.shape[0]):
            gates[n, r:r + 1, :] = in_gates[r, n:n + 1, :]
        copies.append(pltpu.make_async_copy(gates.at[n], out, sems.at[4 + n]))
        copies[-1].start()
    for copy in copies:
        copy.wait()


def shards(cfg, queries, key_inputs, values, beta_gates, log_decay, out_grad):
    X, Q, J, Y = cfg
    heads, lanes = X * Q, 2 * X
    rows_dev = L // lanes
    nb = Q // 2
    slots = nb * lanes
    vmem = pl.BlockSpec(memory_space=pltpu.VMEM)
    hbm = pl.BlockSpec(memory_space=pl.ANY)
    dma = pltpu.SemaphoreType.DMA

    def wide(shape, kind=F32):
        return pltpu.VMEM(shape, kind)

    landed = pl.pallas_call(
        functools.partial(layer_kernel, cfg),
        out_shape=(
            jax.ShapeDtypeStruct((heads, 4 * rows_dev + 16, D), BF16),
            jax.ShapeDtypeStruct((nb, 8, L), F32),
        ),
        in_specs=[hbm] * 6,
        out_specs=(vmem, vmem),
        scratch_shapes=[
            *[wide((1, rows_dev, heads * D), BF16)] * 4, wide((nb, L)), wide((nb, L)),
            *[wide((heads, 2 * rows_dev, D), BF16)] * 2, *[wide((slots, 2 * rows_dev, D), BF16)] * 2,
            wide((nb, 8, L)), wide((nb, 8, L)), wide((3, D, D)), wide((3, D, D)),
            wide((J, 2 * D + 16, D), BF16), wide((J, D + 16, D), BF16),
            *[wide((J, 2 * D, D))] * 2, *[wide((2, D, D))] * 2, *[wide((2 * D + 16, D), BF16)] * 2,
            *[wide((Y, 2 * D + 16, D), BF16)] * 2, *[wide((D, D))] * 2, wide((2, D, D)), wide((2, D, D)),
            wide((slots, 4 * rows_dev + 16, D), BF16), wide((nb, 8, L)),
            dma((6,)), dma((3,)), dma((3,)), dma((2,)), dma((2,)),
            dma((2, J - 1)), dma((2, J - 1)), dma((Y - 1,)), dma((Y - 1,)), dma((2,)), dma((2,)),
        ],
        compiler_params=pltpu.CompilerParams(
            collective_id=0, has_side_effects=True, vmem_limit_bytes=56 * 1024 * 1024),
        name="delta_rule",
    )(queries, key_inputs, values, out_grad, beta_gates, log_decay)
    rows = jax.ShapeDtypeStruct((1, rows_dev, heads * D), F32)
    gates = jax.ShapeDtypeStruct((nb, L), F32)
    return pl.pallas_call(
        unpack_kernel,
        out_shape=(jax.ShapeDtypeStruct(rows.shape, BF16), rows, rows, rows, gates, gates),
        in_specs=[hbm] * 2,
        out_specs=(hbm,) * 6,
        scratch_shapes=[
            wide((heads, 4 * rows_dev + 16, D), BF16), wide((nb, 8, L)),
            wide((rows_dev, heads * D), BF16), wide((3, rows_dev, heads * D)), wide((2, nb, L)),
            dma((2,)), dma((6,))],
        compiler_params=pltpu.CompilerParams(vmem_limit_bytes=56 * 1024 * 1024),
        name="unpack",
    )(*landed)


def build(mesh, y_chips):
    X = mesh.shape["head"] // 2
    heads = 16 if y_chips == 4 else 4 * X
    Q = heads // X
    J = mesh.shape["seq"] // (y_chips * Q)
    rows = P("seq", "head", None)
    gates = P("head", "seq")
    return jax.shard_map(
        functools.partial(shards, (X, Q, J, y_chips)), mesh=mesh,
        in_specs=(rows, rows, rows, gates, gates, rows),
        out_specs=(rows, rows, rows, rows, gates, gates), check_vma=False)


def solution(mesh):
    return build(mesh, 4)
```
